256 devices in a mesh: grid: 64 (over z, y, core), orb: 4 (over x).
Axes of the slice: x: 4, y: 4, z: 8, core: 2. Of those that a mesh axis runs over, the one named last changes fastest.
Arguments:
- c_old: float32 [1024, 65536], P('orb', 'grid'), may hold values from -7 to 7
- c_trial: float32 [1024, 65536], P('orb', 'grid'), may hold values from -7 to 7
Outputs:
- c_new: float32 [1024, 65536], P('orb', 'grid')
- multiplier: float32 [1024, 1024], P('grid', 'orb')
The draws below stay inside these ranges and needn't reach their ends.
All inputs are finite; a program needn't handle non-finite values.
Results may differ from the reference program's by a relative error of at most 0.0001.
Values sent between devices are 32-bit elements; how exact they have to be, the bound alone decides.
No kernel may reach another device: no remote copies, remote signals or barrier semaphores. Data moves between devices by JAX's collectives and lax.ppermute only.
A program may use at most 64 MiB of HBM per device.

```python
import jax
import jax.numpy as jnp
from jax import lax

NORB = 1024
ITERS = 4
NPW = 65536


def field_pair(key):
    first_normal = jnp.clip(jax.random.normal(jax.random.fold_in(key, 1), (NORB, NPW), jnp.float32), -6.0, 6.0)
    second_normal = jnp.clip(jax.random.normal(jax.random.fold_in(key, 3), (NORB, NPW), jnp.float32), -6.0, 6.0)
    along = jax.random.uniform(jax.random.fold_in(key, 5), (NORB, 1), jnp.float32, 0.1, 0.3)
    fresh = jax.random.uniform(jax.random.fold_in(key, 6), (NORB, 1), jnp.float32, 0.6, 0.78)
    first = first_normal
    second = second_normal
    return (first, along * first + fresh * second)


def draw_c_old(key, part):
    previous, trial = field_pair(key)
    return previous


def draw_c_trial(key, part):
    previous, trial = field_pair(key)
    return trial


def setup_inputs(seed: int = 0) -> dict:
    arg_keys = jax.random.split(jax.random.key(seed), 3)
    return {
        "c_old": draw_c_old(jax.random.fold_in(arg_keys[2], 71), 0),
        "c_trial": draw_c_trial(jax.random.fold_in(arg_keys[2], 71), 0),
    }


def product(left, right):
    return jnp.dot(left, right, precision=lax.Precision.HIGHEST, preferred_element_type=jnp.float32)


def reference(c_old, c_trial):
    inverse = 1.0 / NPW
    trial_trial = product(c_trial, c_trial.T) * inverse
    old_trial = product(c_old, c_trial.T) * inverse
    trial_old = old_trial.T
    old_old = product(c_old, c_old.T) * inverse
    identity = jnp.eye(NORB, dtype=jnp.float32)
    multiplier = jnp.zeros((NORB, NORB), jnp.float32)
    for sweep in range(ITERS):
        product_sx = product(old_old, multiplier)
        multiplier = 0.5 * (identity - trial_trial + product(multiplier, identity - old_trial)
                            + product(identity - trial_old, multiplier) - product(multiplier, product_sx))
    c_new = c_trial + product(multiplier.T, c_old)
    return c_new, multiplier
```

```python
import jax
import jax.numpy as jnp
from jax import lax
from jax.sharding import Mesh, PartitionSpec as P

ITERS = 4
NX, NY, NZ, NC = 4, 4, 8, 2
HIGH = lax.Precision.HIGH


def product(left, right, dims=((1,), (0,))):
    return lax.dot_general(
        left, right, (dims, ((), ())), precision=HIGH, preferred_element_type=jnp.float32
    )


def from_offset(value, axis, size, offset):
    return lax.ppermute(value, axis, [((i + offset) % size, i) for i in range(size)])


def ring_gather(value, axis, size):
    return [value] + [from_offset(value, axis, size, r) for r in range(1, size)]


def to_tiles(matrix):
    rows, cols = matrix.shape
    return (
        matrix.reshape(rows // 8, 8, cols // 128, 128)
        .transpose(0, 2, 1, 3)
        .reshape(rows * cols // 1024, 8, 128)
    )


def from_tiles(tiles, cols):
    rows = tiles.shape[0] * 1024 // cols
    return (
        tiles.reshape(rows // 8, cols // 128, 8, 128).transpose(0, 2, 1, 3).reshape(rows, cols)
    )


def reduce_over_grid(tiles):
    count = tiles.shape[0]
    core = lax.axis_index("core")
    half = count // NC
    keep = lax.dynamic_slice_in_dim(tiles, core * half, half, 0)
    send = lax.dynamic_slice_in_dim(tiles, (1 - core) * half, half, 0)
    tiles = keep + from_offset(send, "core", NC, 1)
    for axis, size in (("y", NY), ("z", NZ)):
        tiles = tiles.reshape((size, tiles.shape[0] // size) + tiles.shape[1:])
        tiles = jnp.sum(lax.all_to_all(tiles, axis, 0, 0), axis=0)
    return tiles


def gather_over_z(tiles):
    spread = jnp.broadcast_to(tiles[None], (NZ,) + tiles.shape)
    return lax.all_to_all(spread, "z", 0, 0).reshape((-1,) + tiles.shape[1:])


def gather_over_y(tiles):
    parts = ring_gather(tiles, "y", NY)
    place = lax.axis_index("y")
    stacked = jnp.stack(parts)
    ordered = jnp.concatenate([stacked, stacked])
    return lax.dynamic_slice_in_dim(ordered, (NY - place) % NY, NY, 0).reshape(
        (-1,) + tiles.shape[1:]
    )


def gather_over_core(tiles):
    other = from_offset(tiles, "core", NC, 1)
    first = lax.axis_index("core") == 0
    return jnp.concatenate(
        [jnp.where(first, tiles, other), jnp.where(first, other, tiles)], axis=0
    )


def local(c_old, c_trial):
    block, slab = c_old.shape
    total = block * NX
    inverse = 1.0 / (slab * NC * NY * NZ)
    old_parts = ring_gather(c_old, "x", NX)
    trial_parts = ring_gather(c_trial, "x", NX)
    both = jnp.concatenate([c_trial, c_old], axis=0)
    against = ((1,), (1,))
    es = jnp.concatenate([product(both, part, against) for part in old_parts], axis=1)
    a = jnp.concatenate([product(c_trial, part, against) for part in trial_parts], axis=1)
    partial = jnp.concatenate([a, es], axis=0) * inverse
    mine = gather_over_y(gather_over_z(reduce_over_grid(to_tiles(partial))))
    blocks = []
    for offset, tiles in enumerate(ring_gather(mine, "x", NX)):
        rows = from_tiles(gather_over_core(tiles), total)
        blocks.append(jnp.roll(rows, offset * block, axis=1))
    a, e, s = (
        jnp.concatenate([rows[i * block : (i + 1) * block] for rows in blocks], axis=0)
        for i in range(3)
    )
    identity = jnp.eye(total, dtype=jnp.float32)
    start = identity - a
    x = 0.5 * start
    for sweep in range(ITERS - 2):
        q = product((identity - e) - 0.5 * product(x, s), x)
        x = 0.5 * (start + q + q.T)
    x_col, x_row = x[:, :block], x[:block]
    w_row = (identity - e)[:block] - 0.5 * product(x_row, s)
    q_row = product(w_row, x)
    q_col = x_col - product(e, x_col) - 0.5 * product(x, product(s, x_col))
    x_col = 0.5 * (start[:, :block] + q_col + q_row.T)
    old_all = jnp.concatenate(old_parts, axis=0)
    c_new = c_trial + product(x_col, old_all, ((0,), (0,)))
    grid_place = (lax.axis_index("z") * NY + lax.axis_index("y")) * NC + lax.axis_index("core")
    tile_rows = total // (NZ * NY * NC)
    first = (grid_place * tile_rows - lax.axis_index("x") * block) % total
    return c_new, lax.dynamic_slice_in_dim(x_col, first, tile_rows, 0)


def solution(mesh):
    fine = Mesh(mesh.devices.reshape(NZ, NY, NC, NX), ("z", "y", "core", "x"))
    grid = ("z", "y", "core")
    return jax.shard_map(
        local,
        mesh=fine,
        in_specs=(P("x", grid), P("x", grid)),
        out_specs=(P("x", grid), P(grid, "x")),
        check_vma=False,
    )
```

```python
import jax
import jax.numpy as jnp
from jax import lax
from jax.sharding import Mesh, PartitionSpec as P

ITERS = 4
NX, NY, NZ, NC = 4, 4, 8, 2
HIGH = lax.Precision.HIGH


def product(left, right, dims=((1,), (0,))):
    return lax.dot_general(
        left, right, (dims, ((), ())), precision=HIGH, preferred_element_type=jnp.float32
    )


def against(left, right):
    return product(left, right, ((1,), (1,)))


def from_offset(value, axis, size, offset):
    return lax.ppermute(value, axis, [((i + offset) % size, i) for i in range(size)])


def ring_gather(value, axis, size):
    return [value] + [from_offset(value, axis, size, r) for r in (1, size - 1, 2)]


def halves(value):
    half = value.shape[0] // 2
    core = lax.axis_index("core")
    keep = lax.dynamic_slice_in_dim(value, core * half, half, 0)
    send = lax.dynamic_slice_in_dim(value, (1 - core) * half, half, 0)
    return keep + from_offset(send, "core", NC, 1)


def in_order(parts):
    place = lax.axis_index("y")
    first = parts[0]
    out = jnp.zeros((NY,) + first.shape, first.dtype)
    for offset, part in zip((0, 1, NY - 1, 2), parts):
        out = lax.dynamic_update_slice_in_dim(out, part[None], (place + offset) % NY, 0)
    return out


def gram_parts(c_old, c_trial):
    block, slab = c_old.shape
    quarter = slab // NX
    place = lax.axis_index("x")
    turned = lax.dynamic_slice_in_dim(
        jnp.concatenate([c_trial, c_trial], axis=1), place * quarter, slab, 1
    )
    old_next = from_offset(c_old, "x", NX, 1)
    old_last = from_offset(c_old, "x", NX, -1)
    trial_next = from_offset(turned[:, : 2 * quarter], "x", NX, 1)
    trial_last = from_offset(
        jnp.concatenate([turned[:, 2 * quarter :], turned[:, :quarter]], axis=1), "x", NX, -1
    )
    both = jnp.concatenate([c_trial, c_old], axis=0)
    es = {0: against(both, c_old)}
    es[1] = against(both, old_next)
    es[3] = against(both, old_last)
    half = block // 2
    up, down, es[0], es[1], es[3] = lax.optimization_barrier(
        (old_next[:half], old_last[half:], es[0], es[1], es[3])
    )
    old_far = jnp.concatenate(
        [from_offset(up, "x", NX, 1), from_offset(down, "x", NX, -1)], axis=0
    )
    es[2] = against(both, old_far)
    right = against(turned[:, quarter : 3 * quarter], trial_next)
    left = against(turned[:, 2 * quarter :], trial_last[:, quarter:])
    cross = against(trial_last[:, : 2 * quarter], trial_next)
    mine = 0.5 * against(c_trial, c_trial)
    a = jnp.concatenate([mine, right, cross, left], axis=1)
    return [c_old, old_next, old_far, old_last], a, [es[r] for r in range(NX)]


def reduce_over_grid(a, es, inverse):
    es = jnp.concatenate([halves(part) for part in es], axis=1)
    a = halves(a)
    cols = a.shape[1]
    rows = jnp.concatenate(
        [es.reshape(NY, es.shape[0] // NY, cols), a.reshape(NY, a.shape[0] // NY, cols)], axis=1
    )
    rows = jnp.sum(lax.all_to_all(rows, "y", 0, 0), axis=0)
    count = rows.shape[0]
    tiles = rows.reshape(count, NZ, cols // NZ).transpose(1, 0, 2)
    return jnp.sum(lax.all_to_all(tiles, "z", 0, 0), axis=0) * inverse


def gather_over_z(tile):
    return lax.all_to_all(jnp.broadcast_to(tile[None], (NZ,) + tile.shape), "z", 0, 0)


def other_core(value):
    return from_offset(value, "core", NC, 1)


def ring_order(parts):
    return [parts[0], parts[1], parts[3], parts[2]]


def gather_all(tile):
    tiles = gather_over_z(tile)
    first, second = tiles[: NZ // 2], tiles[NZ // 2 :]
    first_y = ring_gather(first, "y", NY)
    second_x = ring_gather(second, "x", NX)
    first = in_order(first_y)
    second = jnp.stack(ring_order(second_x))
    first_parts = ring_order(ring_gather(first, "x", NX))
    second_parts = ring_gather(second, "y", NY)
    first_other = [other_core(part) for part in first_parts]
    second_other = [other_core(part) for part in second_parts]
    out = []
    for x_parts, y_parts in ((first_parts, second_parts), (first_other, second_other)):
        one = jnp.stack(x_parts)
        two = in_order(y_parts).transpose(1, 0, 2, 3, 4)
        out.append(jnp.concatenate([one, two], axis=2))
    return out


def to_rows(value):
    r, y, tiles, rows, lanes = value.shape
    return value.transpose(0, 1, 3, 2, 4).reshape(r, y * rows, tiles * lanes)


def unroll(value):
    r, rows, cols = value.shape
    return jnp.concatenate(
        [jnp.roll(value[i], i * (cols // NX), axis=1) for i in range(r)], axis=0
    )


def local(c_old, c_trial):
    block, slab = c_old.shape
    total = block * NX
    old_parts, a, es = gram_parts(c_old, c_trial)
    tile = reduce_over_grid(a, es, 1.0 / (slab * NC * NY * NZ))
    own, other = gather_all(tile)
    first = lax.axis_index("core") == 0
    split = block // NY
    e = unroll(to_rows(jnp.where(first, own[:, :, :, :split], other[:, :, :, :split])))
    s = unroll(to_rows(jnp.where(first, other[:, :, :, :split], own[:, :, :, :split])))
    own_n, other_n = to_rows(own[:, :, :, split:]), to_rows(other[:, :, :, split:])
    n = jnp.concatenate(
        [jnp.where(first, own_n, other_n), jnp.where(first, other_n, own_n)], axis=1
    )
    far = slice(2 * block, 3 * block)
    n = jnp.concatenate(
        [n[:, :, : 2 * block], jnp.roll(n[:, :, far], -1, axis=0), n[:, :, 3 * block :]], axis=2
    )
    n = unroll(n)
    identity = jnp.eye(total, dtype=jnp.float32)
    start = identity - (n + n.T)
    x = 0.5 * start
    for sweep in range(ITERS - 2):
        q = product((identity - e) - 0.5 * product(x, s), x)
        x = 0.5 * (start + q + q.T)
    x_row = x[:block]
    w_row = (identity - e)[:block] - product(x_row, s)
    x_row = 0.5 * (start[:block] + x_row + product(w_row, x) - against(x_row, e))
    old_all = jnp.concatenate(old_parts, axis=0)
    c_new = c_trial + product(x_row, old_all)
    grid_place = (lax.axis_index("z") * NY + lax.axis_index("y")) * NC + lax.axis_index("core")
    tile_rows = total // (NZ * NY * NC)
    begin = (grid_place * tile_rows - lax.axis_index("x") * block) % total
    return c_new, lax.dynamic_slice_in_dim(x_row.T, begin, tile_rows, 0)


def solution(mesh):
    fine = Mesh(mesh.devices.reshape(NZ, NY, NC, NX), ("z", "y", "core", "x"))
    grid = ("z", "y", "core")
    return jax.shard_map(
        local,
        mesh=fine,
        in_specs=(P("x", grid), P("x", grid)),
        out_specs=(P("x", grid), P(grid, "x")),
        check_vma=False,
    )
```

```python
import functools

import jax
import jax.numpy as jnp
from jax import lax
from jax.experimental import pallas as pl
from jax.experimental.pallas import tpu as pltpu
from jax.sharding import Mesh, PartitionSpec as P

ITERS = 4
NX, NY, NZ, NC = 4, 4, 8, 2
HIGH = lax.Precision.HIGH
BF16, F32 = jnp.bfloat16, jnp.float32
VMEM_BYTES = 56 * 1024 * 1024


def product(left, right, dims=((1,), (0,))):
    return lax.dot_general(
        left, right, (dims, ((), ())), precision=HIGH, preferred_element_type=jnp.float32
    )


def against(left, right):
    return product(left, right, ((1,), (1,)))


def from_offset(value, axis, size, offset):
    return lax.ppermute(value, axis, [((i + offset) % size, i) for i in range(size)])


def ring_gather(value, axis, size):
    return [value] + [from_offset(value, axis, size, r) for r in (1, size - 1, 2)]


def halves(value):
    half = value.shape[0] // 2
    core = lax.axis_index("core")
    keep = lax.dynamic_slice_in_dim(value, core * half, half, 0)
    send = lax.dynamic_slice_in_dim(value, (1 - core) * half, half, 0)
    return keep + from_offset(send, "core", NC, 1)


def gram_parts(c_old, c_trial):
    block, slab = c_old.shape
    quarter = slab // NX
    place = lax.axis_index("x")
    turned = lax.dynamic_slice_in_dim(
        jnp.concatenate([c_trial, c_trial], axis=1), place * quarter, slab, 1
    )
    old_next = from_offset(c_old, "x", NX, 1)
    old_last = from_offset(c_old, "x", NX, -1)
    half = block // 2
    both = jnp.concatenate([c_trial, c_old], axis=0)
    es = {0: against(both, c_old)}
    to_last = turned[:, : 2 * quarter]
    to_next = jnp.concatenate([turned[:, 2 * quarter :], turned[:, :quarter]], axis=1)
    old_next, old_last, to_last, to_next, es[0] = lax.optimization_barrier(
        (old_next, old_last, to_last, to_next, es[0])
    )
    up = from_offset(old_next[:half], "x", NX, 1)
    down = from_offset(old_last[half:], "x", NX, -1)
    trial_next = from_offset(to_last, "x", NX, 1)
    trial_last = from_offset(to_next, "x", NX, -1)
    es[1] = against(both, old_next)
    es[3] = against(both, old_last)
    old_far = jnp.concatenate([up, down], axis=0)
    es[2] = against(both, old_far)
    right = against(turned[:, quarter : 3 * quarter], trial_next)
    left = against(turned[:, 2 * quarter :], trial_last[:, quarter:])
    cross = against(trial_last[:, : 2 * quarter], trial_next)
    mine = 0.5 * against(c_trial, c_trial)
    a = jnp.concatenate([mine, right, cross, left], axis=1)
    return [c_old, old_next, old_far, old_last], a, [es[r] for r in range(NX)]


def reduce_over_grid(a, es, inverse):
    es = jnp.concatenate([halves(part) for part in es], axis=1)
    a = halves(a)
    cols = a.shape[1]
    rows = jnp.concatenate(
        [es.reshape(NY, es.shape[0] // NY, cols), a.reshape(NY, a.shape[0] // NY, cols)], axis=1
    )
    rows = jnp.sum(lax.all_to_all(rows, "y", 0, 0), axis=0)
    count = rows.shape[0]
    tiles = rows.reshape(count, NZ, cols // NZ).transpose(1, 0, 2)
    return jnp.sum(lax.all_to_all(tiles, "z", 0, 0), axis=0) * inverse


def gather_over_z(tile):
    return lax.all_to_all(jnp.broadcast_to(tile[None], (NZ,) + tile.shape), "z", 0, 0)


def other_core(value):
    return from_offset(value, "core", NC, 1)


def ring_order(parts):
    return [parts[0], parts[1], parts[3], parts[2]]


def gather_all(tile):
    tiles = gather_over_z(tile)
    first, second = tiles[: NZ // 2], tiles[NZ // 2 :]
    first = jnp.stack(ring_order(ring_gather(first, "y", NY)))
    second = jnp.stack(ring_order(ring_gather(second, "x", NX)))
    first, second = lax.optimization_barrier((first, second))
    first_parts = ring_order(ring_gather(first, "x", NX))
    second_parts = ring_order(ring_gather(second, "y", NY))
    pieces = first_parts + second_parts
    return pieces, [other_core(part) for part in pieces]


def split(value):
    high = value.astype(BF16)
    return high, (value - high.astype(F32)).astype(BF16)


def dot(left, right):
    return jnp.dot(left, right, preferred_element_type=F32)


def dot_nt(left, right):
    return lax.dot_general(left, right, (((1,), (1,)), ((), ())), preferred_element_type=F32)


def three(left, right, form=dot):
    return form(left[0], right[0]) + (form(left[0], right[1]) + form(left[1], right[0]))


def constrain(place, *refs, block):
    own, other = refs[: NX + NY], refs[NX + NY : 2 * (NX + NY)]
    olds = refs[2 * (NX + NY) : 2 * (NX + NY) + NX]
    trial, c_new, mult = refs[2 * (NX + NY) + NX : 2 * (NX + NY) + NX + 3]
    es, n, xh, xl, sh, sl, wh, wl, q = refs[2 * (NX + NY) + NX + 3 :]
    total = NX * block
    y, core = place[0], place[1]
    es_rows, n_rows = block // NY, block // NY // NC
    lanes = total // NZ
    tiles = NZ // 2

    def put(ref, pair, at, shift, turn, tile, first_tile):
        which = core if pair == 0 else 1 - core
        column = (shift * block + (first_tile + tile) * lanes) % total
        wide = slice(column, column + lanes)
        group = lax.rem(y + turn, NY)
        value = ref[at, tile]
        es[which, pl.ds(shift * block + group * es_rows, es_rows), wide] = value[:es_rows]
        if (first_tile + tile) * lanes // block == 2:
            shift = (shift - 1) % NX
            column = (column - block) % total
            wide = slice(column, column + lanes)
        row = shift * block + which * (NY * n_rows) + group * n_rows
        n[pl.ds(row, n_rows), wide] = value[es_rows:]

    for pair, parts in enumerate((own, other)):
        for shift in range(NX):
            for turn in range(NY):
                for tile in range(tiles):
                    put(parts[shift], pair, turn, shift, turn, tile, 0)
                    put(parts[NX + turn], pair, shift, shift, turn, tile, tiles)

    def eye():
        rows = lax.broadcasted_iota(jnp.int32, (block, block), 0)
        cols = lax.broadcasted_iota(jnp.int32, (block, block), 1)
        return (rows == cols).astype(F32)

    def span(i):
        return slice(i * block, (i + 1) * block)

    for i in range(NX):
        es[0, span(i), span(i)] = es[0, span(i), span(i)] - eye()
        for j in range(i + 1):
            a = n[span(i), span(j)] + n[span(j), span(i)].T
            start = (eye() - a) if i == j else -a
            n[span(i), span(j)] = start
            high, low = split(0.5 * start)
            xh[span(i), span(j)], xl[span(i), span(j)] = high, low
            if i != j:
                start = start.T
                n[span(j), span(i)] = start
                high, low = split(0.5 * start)
                xh[span(j), span(i)], xl[span(j), span(i)] = high, low
        high, low = split(es[1, span(i)])
        sh[span(i)], sl[span(i)] = high, low

    def columns(i):
        return pl.ds(pl.multiple_of(i * block, block), block)

    for sweep in range(ITERS - 2):

        def inner(i, carry):
            cols = columns(i)
            value = three((xh[...], xl[...]), (sh[:, cols], sl[:, cols]))
            high, low = split(-es[0, :, cols] - 0.5 * value)
            wh[:, cols], wl[:, cols] = high, low
            return carry

        lax.fori_loop(0, NX, inner, 0)

        def outer(i, carry):
            cols = columns(i)
            q[:total, cols] = three((wh[...], wl[...]), (xh[:, cols], xl[:, cols]))
            return carry

        lax.fori_loop(0, NX, outer, 0)
        for i in range(NX):
            for j in range(i + 1):
                value = 0.5 * (n[span(i), span(j)] + (q[span(i), span(j)] + q[span(j), span(i)].T))
                high, low = split(value)
                xh[span(i), span(j)], xl[span(i), span(j)] = high, low
                if i != j:
                    high, low = split(value.T)
                    xh[span(j), span(i)], xl[span(j), span(i)] = high, low

    row = (xh[:block], xl[:block])
    for j in range(NX):
        value = three(row, (sh[:, span(j)], sl[:, span(j)]))
        high, low = split(-es[0, :block, span(j)] - value)
        wh[:block, span(j)], wl[:block, span(j)] = high, low
    weight = (wh[:block], wl[:block])
    for j in range(NX):
        value = three(weight, (xh[:, span(j)], xl[:, span(j)]))
        value = value - three(row, split(es[0, span(j)]), dot_nt)
        q[:block, span(j)] = 0.5 * (n[:block, span(j)] + value)
    for j in range(NX):
        high, low = split(q[:block, span(j)])
        wh[:block, span(j)], wl[:block, span(j)] = high, low
        q[pl.ds(block + j * block, block), :block] = q[:block, span(j)].T
    begin = place[2]
    mult[...] = q[pl.ds(pl.multiple_of(block + begin, 16), mult.shape[0]), :block]
    value = trial[...]
    for j in range(NX):
        value = value + three((wh[:block, span(j)], wl[:block, span(j)]), split(olds[j][...]))
    c_new[...] = value


def local(c_old, c_trial):
    block, slab = c_old.shape
    total = block * NX
    old_parts, a, es = gram_parts(c_old, c_trial)
    tile = reduce_over_grid(a, es, 1.0 / (slab * NC * NY * NZ))
    own, other = gather_all(tile)
    y, core = lax.axis_index("y"), lax.axis_index("core")
    grid_place = (lax.axis_index("z") * NY + y) * NC + core
    tile_rows = total // (NZ * NY * NC)
    begin = (grid_place * tile_rows - lax.axis_index("x") * block) % total
    place = jnp.stack([y, core, begin]).astype(jnp.int32)
    vmem = pl.BlockSpec(memory_space=pltpu.VMEM)
    wide = pltpu.VMEM((total, total), F32)
    thin = pltpu.VMEM((total, total), BF16)
    count = 2 * (NX + NY) + NX + 1
    return pl.pallas_call(
        functools.partial(constrain, block=block),
        out_shape=(
            jax.ShapeDtypeStruct((block, slab), F32),
            jax.ShapeDtypeStruct((tile_rows, block), F32),
        ),
        in_specs=[pl.BlockSpec(memory_space=pltpu.SMEM)] + [vmem] * count,
        out_specs=(vmem, vmem),
        scratch_shapes=[pltpu.VMEM((2, total, total), F32), wide]
        + [thin] * 6
        + [pltpu.VMEM((total + block, total), F32)],
        compiler_params=pltpu.CompilerParams(vmem_limit_bytes=VMEM_BYTES),
        cost_estimate=pl.CostEstimate(
            flops=40 * total**3, bytes_accessed=24 * 1024 * 1024, transcendentals=0
        ),
    )(place, *own, *other, *old_parts, c_trial)


def solution(mesh):
    fine = Mesh(mesh.devices.reshape(NZ, NY, NC, NX), ("z", "y", "core", "x"))
    grid = ("z", "y", "core")
    return jax.shard_map(
        local,
        mesh=fine,
        in_specs=(P("x", grid), P("x", grid)),
        out_specs=(P("x", grid), P(grid, "x")),
        check_vma=False,
    )
```

```python
import functools

import jax
import jax.numpy as jnp
from jax import lax
from jax.experimental import pallas as pl
from jax.experimental.pallas import tpu as pltpu
from jax.sharding import Mesh, PartitionSpec as P

ITERS = 4
NX, NY, NZ, NC = 4, 4, 8, 2
HIGH = lax.Precision.HIGH
BF16, F32 = jnp.bfloat16, jnp.float32
VMEM_BYTES = 56 * 1024 * 1024


def product(left, right, dims=((1,), (0,))):
    return lax.dot_general(
        left, right, (dims, ((), ())), precision=HIGH, preferred_element_type=jnp.float32
    )


def against(left, right):
    return product(left, right, ((1,), (1,)))


def from_offset(value, axis, size, offset):
    return lax.ppermute(value, axis, [((i + offset) % size, i) for i in range(size)])


def ring_gather(value, axis, size):
    return [value] + [from_offset(value, axis, size, r) for r in range(1, size)]


def ring_forward(value, axis, size):
    half = value.shape[0] // 2
    after = from_offset(value, axis, size, 1)
    before = from_offset(value, axis, size, -1)
    top = from_offset(after[:half], axis, size, 1)
    low = from_offset(before[half:], axis, size, -1)
    return [value, after, top, low, before]


def other_core(value):
    return from_offset(value, "core", NC, 1)


def halves(value):
    half = value.shape[0] // 2
    core = lax.axis_index("core")
    keep = lax.dynamic_slice_in_dim(value, core * half, half, 0)
    send = lax.dynamic_slice_in_dim(value, (1 - core) * half, half, 0)
    return keep + other_core(send)


def row_tiles(value):
    rows, cols = value.shape
    return value.reshape(NY, NZ, rows // NY // NZ, cols // 128, 128).transpose(0, 1, 3, 2, 4)


def column_tiles(value):
    rows, cols = value.shape
    return value.reshape(NY, rows // NY // 8, 8, NZ, cols // NZ).transpose(0, 3, 1, 2, 4)


def sum_over_zy(tiles):
    tiles = jnp.sum(lax.all_to_all(tiles, "y", 0, 0), axis=0)
    return jnp.sum(lax.all_to_all(tiles, "z", 0, 0), axis=0)


def gram_tiles(c_old, c_trial):
    block, slab = c_old.shape
    quarter = slab // NX
    place = lax.axis_index("x")
    old_next = from_offset(c_old, "x", NX, 1)
    old_last = from_offset(c_old, "x", NX, -1)
    turned = lax.dynamic_slice_in_dim(
        jnp.concatenate([c_trial, c_trial], axis=1), place * quarter, slab, 1
    )
    both = jnp.concatenate([c_trial, c_old], axis=0)
    es_own = against(both, c_old)
    to_last = turned[:, : 2 * quarter]
    to_next = jnp.concatenate([turned[:, 2 * quarter :], turned[:, :quarter]], axis=1)
    old_next, old_last, to_last, to_next, es_own = lax.optimization_barrier(
        (old_next, old_last, to_last, to_next, es_own)
    )
    half = block // 2
    up, down, old_next, old_last = lax.optimization_barrier(
        (old_next[:half], old_last[half:], old_next, old_last)
    )
    up = from_offset(up, "x", NX, 1)
    down = from_offset(down, "x", NX, -1)
    trial_next = from_offset(to_last, "x", NX, 1)
    trial_last = from_offset(to_next, "x", NX, -1)
    early = jnp.concatenate([es_own, against(both, old_next), against(both, old_last)], axis=1)
    early = sum_over_zy(row_tiles(halves(early)))
    early, up, down, trial_next, trial_last = lax.optimization_barrier(
        (early, up, down, trial_next, trial_last)
    )
    old_far = jnp.concatenate([up, down], axis=0)
    es_far = halves(against(both, old_far))
    right = against(turned[:, quarter : 3 * quarter], trial_next)
    left = against(turned[:, 2 * quarter :], trial_last[:, quarter:])
    cross = against(trial_last[:, : 2 * quarter], trial_next)
    mine = 0.5 * against(c_trial, c_trial)
    a = halves(jnp.concatenate([mine, right, cross, left], axis=1))
    late = sum_over_zy(jnp.concatenate([row_tiles(es_far), column_tiles(a)], axis=2))
    return [c_old, old_next, old_far, old_last], jnp.concatenate([early, late], axis=0)


def gather_over_z(tile):
    return lax.all_to_all(jnp.broadcast_to(tile[None], (NZ,) + tile.shape), "z", 0, 0)


def gather_all(tile):
    tiles = gather_over_z(tile)
    first, second = tiles[: NZ // 2], tiles[NZ // 2 :]
    first = jnp.stack(ring_gather(first, "y", NY))
    second = jnp.stack(ring_gather(second, "x", NX))
    first, second = lax.optimization_barrier((first, second))
    pieces = ring_forward(first, "x", NX) + ring_forward(second, "y", NY)
    return pieces, [other_core(part) for part in pieces]


def split(value):
    high = value.astype(BF16)
    return high, (value - high.astype(F32)).astype(BF16)


def dot(left, right):
    return jnp.dot(left, right, preferred_element_type=F32)


def dot_nt(left, right):
    return lax.dot_general(left, right, (((1,), (1,)), ((), ())), preferred_element_type=F32)


def three(left, right, form=dot):
    return form(left[0], right[0]) + (form(left[0], right[1]) + form(left[1], right[0]))


PIECES = 5
EARLY = (0, 1, 3)


def constrain(place, *refs, block):
    count = 2 * PIECES
    own, other = refs[:count], refs[count : 2 * count]
    olds = refs[2 * count : 2 * count + NX]
    trial, c_new, mult = refs[2 * count + NX : 2 * count + NX + 3]
    es, n, xh, xl, sh, sl, wh, wl, q = refs[2 * count + NX + 3 :]
    total = NX * block
    y, core = place[0], place[1]
    es_rows, n_rows = block // NY, block // NY // NC
    lanes = 128
    wide = block // lanes
    early = len(EARLY) * wide

    def put(value, which, shift, turn, z):
        group = lax.rem(y + turn, NY)

        def at(column):
            column = column % total
            return slice(column, column + lanes)

        row = shift * block + group * es_rows + z * 8
        for k in range(NX * wide):
            slot = EARLY[k // wide] if k < early else 2
            column = (shift + slot) * block + k % wide * lanes
            es[which, pl.ds(pl.multiple_of(row, 8), 8), at(column)] = value[k]
        column = shift * block + z * lanes
        if z // wide == 2:
            shift = (shift - 1) % NX
            column = column - block
        row = shift * block + which * (NY * n_rows) + group * n_rows
        for k in range(n_rows // 8):
            n[pl.ds(pl.multiple_of(row + 8 * k, 8), 8), at(column)] = value[NX * wide + k]

    def piece(parts, offset, index):
        if offset == 2:
            half = NX // 2
            return parts[2 + index // half], index % half
        return parts[offset if offset < 2 else offset + 1], index

    for pair, parts in enumerate((own, other)):
        which = core if pair == 0 else 1 - core
        for shift in range(NX):
            for turn in range(NY):
                for z in range(NZ):
                    if z < NZ // 2:
                        ref, index = piece(parts[:PIECES], shift, turn)
                    else:
                        ref, index = piece(parts[PIECES:], turn, shift)
                    put(ref[index, z % (NZ // 2)], which, shift, turn, z)

    def eye():
        rows = lax.broadcasted_iota(jnp.int32, (block, block), 0)
        cols = lax.broadcasted_iota(jnp.int32, (block, block), 1)
        return (rows == cols).astype(F32)

    def span(i):
        return slice(i * block, (i + 1) * block)

    for i in range(NX):
        es[0, span(i), span(i)] = es[0, span(i), span(i)] - eye()
        for j in range(i + 1):
            a = n[span(i), span(j)] + n[span(j), span(i)].T
            start = (eye() - a) if i == j else -a
            n[span(i), span(j)] = start
            high, low = split(0.5 * start)
            xh[span(i), span(j)], xl[span(i), span(j)] = high, low
            if i != j:
                start = start.T
                n[span(j), span(i)] = start
                high, low = split(0.5 * start)
                xh[span(j), span(i)], xl[span(j), span(i)] = high, low
        high, low = split(es[1, span(i)])
        sh[span(i)], sl[span(i)] = high, low

    def columns(i):
        return pl.ds(pl.multiple_of(i * block, block), block)

    for sweep in range(ITERS - 2):

        def inner(i, carry):
            cols = columns(i)
            value = three((xh[...], xl[...]), (sh[:, cols], sl[:, cols]))
            high, low = split(-es[0, :, cols] - 0.5 * value)
            wh[:, cols], wl[:, cols] = high, low
            return carry

        lax.fori_loop(0, NX, inner, 0)

        def outer(i, carry):
            cols = columns(i)
            q[:total, cols] = three((wh[...], wl[...]), (xh[:, cols], xl[:, cols]))
            return carry

        lax.fori_loop(0, NX, outer, 0)
        for i in range(NX):
            for j in range(i + 1):
                value = 0.5 * (n[span(i), span(j)] + (q[span(i), span(j)] + q[span(j), span(i)].T))
                high, low = split(value)
                xh[span(i), span(j)], xl[span(i), span(j)] = high, low
                if i != j:
                    high, low = split(value.T)
                    xh[span(j), span(i)], xl[span(j), span(i)] = high, low

    row = (xh[:block], xl[:block])
    for j in range(NX):
        value = three(row, (sh[:, span(j)], sl[:, span(j)]))
        high, low = split(-es[0, :block, span(j)] - value)
        wh[:block, span(j)], wl[:block, span(j)] = high, low
    weight = (wh[:block], wl[:block])
    for j in range(NX):
        value = three(weight, (xh[:, span(j)], xl[:, span(j)]))
        value = value - three(row, split(es[0, span(j)]), dot_nt)
        q[:block, span(j)] = 0.5 * (n[:block, span(j)] + value)
    for j in range(NX):
        high, low = split(q[:block, span(j)])
        wh[:block, span(j)], wl[:block, span(j)] = high, low
        q[pl.ds(block + j * block, block), :block] = q[:block, span(j)].T
    begin = place[2]
    mult[...] = q[pl.ds(pl.multiple_of(block + begin, 16), mult.shape[0]), :block]
    value = trial[...]
    for j in range(NX):
        value = value + three((wh[:block, span(j)], wl[:block, span(j)]), split(olds[j][...]))
    c_new[...] = value


def local(c_old, c_trial):
    block, slab = c_old.shape
    total = block * NX
    old_parts, tile = gram_tiles(c_old, c_trial)
    own, other = gather_all(tile * (1.0 / (slab * NC * NY * NZ)))
    y, core = lax.axis_index("y"), lax.axis_index("core")
    grid_place = (lax.axis_index("z") * NY + y) * NC + core
    tile_rows = total // (NZ * NY * NC)
    begin = (grid_place * tile_rows - lax.axis_index("x") * block) % total
    place = jnp.stack([y, core, begin]).astype(jnp.int32)
    vmem = pl.BlockSpec(memory_space=pltpu.VMEM)
    wide = pltpu.VMEM((total, total), F32)
    thin = pltpu.VMEM((total, total), BF16)
    count = 4 * PIECES + NX + 1
    return pl.pallas_call(
        functools.partial(constrain, block=block),
        out_shape=(
            jax.ShapeDtypeStruct((block, slab), F32),
            jax.ShapeDtypeStruct((tile_rows, block), F32),
        ),
        in_specs=[pl.BlockSpec(memory_space=pltpu.SMEM)] + [vmem] * count,
        out_specs=(vmem, vmem),
        scratch_shapes=[pltpu.VMEM((2, total, total), F32), wide]
        + [thin] * 6
        + [pltpu.VMEM((total + block, total), F32)],
        compiler_params=pltpu.CompilerParams(vmem_limit_bytes=VMEM_BYTES),
        cost_estimate=pl.CostEstimate(
            flops=40 * total**3, bytes_accessed=24 * 1024 * 1024, transcendentals=0
        ),
    )(place, *own, *other, *old_parts, c_trial)


def solution(mesh):
    fine = Mesh(mesh.devices.reshape(NZ, NY, NC, NX), ("z", "y", "core", "x"))
    grid = ("z", "y", "core")
    return jax.shard_map(
        local,
        mesh=fine,
        in_specs=(P("x", grid), P("x", grid)),
        out_specs=(P("x", grid), P(grid, "x")),
        check_vma=False,
    )
```

```python
import functools

import jax
import jax.numpy as jnp
from jax import lax
from jax.experimental import pallas as pl
from jax.experimental.pallas import tpu as pltpu
from jax.sharding import Mesh, PartitionSpec as P

ITERS = 4
NX, NY, NZ, NC = 4, 4, 8, 2
BF16, F32 = jnp.bfloat16, jnp.float32
PIECES = 5
SLOTS = 6
VMEM_BYTES = 56 * 1024 * 1024


def from_offset(value, axis, size, offset):
    return lax.ppermute(value, axis, [((i + offset) % size, i) for i in range(size)])


def ring_gather(value, axis, size):
    return [value] + [from_offset(value, axis, size, r) for r in range(1, size)]


def ring_forward(value, axis, size):
    half = value.shape[0] // 2
    after = from_offset(value, axis, size, 1)
    before = from_offset(value, axis, size, -1)
    top = from_offset(after[:half], axis, size, 1)
    low = from_offset(before[half:], axis, size, -1)
    return [value, after, top, low, before]


def other_core(value):
    return from_offset(value, "core", NC, 1)


def split(value):
    high = value.astype(BF16)
    return high, (value - high.astype(F32)).astype(BF16)


def dot(left, right):
    return jnp.dot(left, right, preferred_element_type=F32)


def dot_nt(left, right):
    return lax.dot_general(left, right, (((1,), (1,)), ((), ())), preferred_element_type=F32)


def three(left, right, form=dot):
    return form(left[0], right[0]) + (form(left[0], right[1]) + form(left[1], right[0]))


def messages(place, trial, to_last, to_next):
    x = place[3]
    quarter = trial.shape[1] // NX
    for k, (ref, at) in enumerate(((to_last, 0), (to_last, 1), (to_next, 0), (to_next, 1))):
        ref[:, at * quarter : (at + 1) * quarter] = trial[:, quarter_at(x + k, quarter)]
    to_next[:, 2 * quarter :] = trial[:, quarter_at(x, quarter)]


def quarter_at(index, quarter):
    return pl.ds(pl.multiple_of(lax.rem(index, NX) * quarter, quarter), quarter)


def put_block(core, keep, send, slot, value):
    half = value.shape[0] // NC
    first = core == 0
    kept = jnp.where(first, value[:half], value[half:])
    sent = jnp.where(first, value[half:], value[:half])
    wide = value.shape[1] // 128
    deep = NZ // wide
    for y in range(NY):
        for z in range(NZ):
            rows = slice((y * deep + z // wide) * 8, (y * deep + z // wide) * 8 + 8)
            cols = slice(z % wide * 128, z % wide * 128 + 128)
            keep[y, z, slot] = kept[rows, cols]
            send[y, z, slot] = sent[rows, cols]


def near_blocks(place, trial, old, after, before, keep, send):
    core = place[1]
    t, c, a, b = (split(ref[...]) for ref in (trial, old, after, before))
    pairs = ((t, c), (t, a), (t, b), (c, c), (c, a), (t, t))
    for slot, (left, right) in enumerate(pairs):
        put_block(core, keep, send, slot, three(left, right, dot_nt))


def far_blocks(place, trial, trial_after, trial_before, after, before, keep, send):
    core, x = place[1], place[3]
    quarter = trial.shape[1] // NX

    def pair(ref, first):
        parts = [split(ref[:, quarter_at(x + first + k, quarter)]) for k in range(2)]
        return tuple(jnp.concatenate([parts[0][k], parts[1][k]], axis=1) for k in range(2))

    ta = split(trial_after[...])
    tb = split(trial_before[...])
    tb_first = tuple(part[:, : 2 * quarter] for part in tb)
    tb_second = tuple(part[:, quarter:] for part in tb)
    ca, cb = pair(after, 1), pair(before, 1)
    pairs = (
        (tb_first, ca),
        (ta, cb),
        (cb, ca),
        (tb_first, ta),
        (pair(trial, 1), ta),
        (pair(trial, 2), tb_second),
    )
    for slot, (left, right) in enumerate(pairs):
        put_block(core, keep, send, slot, three(left, right, dot_nt))


VMEM = pl.BlockSpec(memory_space=pltpu.VMEM)
SMEM = pl.BlockSpec(memory_space=pltpu.SMEM)


def tile_kernel(body, place, operands, block, flops):
    tiles = jax.ShapeDtypeStruct((NY, NZ, SLOTS, 8, 128), F32)
    keep, send = pl.pallas_call(
        body,
        out_shape=(tiles, tiles),
        in_specs=[SMEM] + [VMEM] * len(operands),
        out_specs=(VMEM, VMEM),
        compiler_params=pltpu.CompilerParams(vmem_limit_bytes=32 * 1024 * 1024),
        cost_estimate=pl.CostEstimate(
            flops=flops, bytes_accessed=6 * 1024 * 1024, transcendentals=0
        ),
    )(place, *operands)
    return keep, other_core(send)


def gram(c_old, c_trial, place):
    block, slab = c_old.shape
    quarter = slab // NX
    after = from_offset(c_old, "x", NX, 1)
    before = from_offset(c_old, "x", NX, -1)
    to_last, to_next = pl.pallas_call(
        messages,
        out_shape=(
            jax.ShapeDtypeStruct((block, 2 * quarter), F32),
            jax.ShapeDtypeStruct((block, 3 * quarter), F32),
        ),
        in_specs=[SMEM, VMEM],
        out_specs=(VMEM, VMEM),
    )(place, c_trial)
    trial_after = from_offset(to_last, "x", NX, 1)
    trial_before = from_offset(to_next, "x", NX, -1)
    flops = 6 * 6 * block * block * slab
    near, near_other = tile_kernel(
        near_blocks, place, (c_trial, c_old, after, before), block, flops
    )
    near, trial_after, trial_before = lax.optimization_barrier((near, trial_after, trial_before))
    far, far_other = tile_kernel(
        far_blocks, place, (c_trial, trial_after, trial_before, after, before), block, flops // 2
    )
    to_far, far = lax.optimization_barrier((c_old, far))
    far_old = from_offset(to_far, "x", NX, 2)
    tiles = jnp.concatenate([near + near_other, far + far_other], axis=2)
    return [c_old, after, far_old, before], tiles


def sum_over(tiles, axis):
    return jnp.sum(lax.all_to_all(tiles, axis, 0, 0), axis=0)


def gather_over_z(tile):
    return lax.all_to_all(jnp.broadcast_to(tile[None], (NZ,) + tile.shape), "z", 0, 0)


def gather_all(tile):
    tiles = gather_over_z(tile)
    first, second = tiles[: NZ // 2], tiles[NZ // 2 :]
    first = jnp.stack(ring_gather(first, "y", NY))
    second = jnp.stack(ring_gather(second, "x", NX))
    first, second = lax.optimization_barrier((first, second))
    pieces = ring_forward(first, "x", NX) + ring_forward(second, "y", NY)
    return pieces, [other_core(part) for part in pieces]


def constrain(place, *refs, block):
    count = 2 * PIECES
    own, other = refs[:count], refs[count : 2 * count]
    olds = refs[2 * count : 2 * count + NX]
    trial, c_new, mult = refs[2 * count + NX : 2 * count + NX + 3]
    e, s, n, xh, xl, sh, sl, wh, wl, q = refs[2 * count + NX + 3 :]
    total = NX * block
    y, core = place[0], place[1]
    lanes = 128
    wide = block // lanes
    core_rows = block // NC
    y_rows = core_rows // NY

    def put(value, which, shift, turn, z):
        group = lax.rem(y + turn, NY)
        inside = which * core_rows + group * y_rows + z // wide * 8
        r, after, before = shift, (shift + 1) % NX, (shift - 1) % NX
        targets = (
            (e, r, r),
            (e, r, after),
            (e, r, before),
            (s, r, r),
            (s, r, after),
            (n, r, r),
            (e, before, after),
            (s, after, r),
            (s, before, after),
            (n, before, after),
            (n, r, after),
            (n, r, before),
        )
        for k, (ref, row, col) in enumerate(targets):
            column = col * block + z % wide * lanes
            row = pl.multiple_of(row * block + inside, 8)
            ref[pl.ds(row, 8), column : column + lanes] = value[k]

    def piece(parts, offset, index):
        if offset == 2:
            half = NX // 2
            return parts[2 + index // half], index % half
        return parts[offset if offset < 2 else offset + 1], index

    for pair, parts in enumerate((own, other)):
        which = core if pair == 0 else 1 - core
        for shift in range(NX):
            for turn in range(NY):
                for z in range(NZ):
                    if z < NZ // 2:
                        ref, index = piece(parts[:PIECES], shift, turn)
                    else:
                        ref, index = piece(parts[PIECES:], turn, shift)
                    put(ref[index, z % (NZ // 2)], which, shift, turn, z)

    def eye():
        rows = lax.broadcasted_iota(jnp.int32, (block, block), 0)
        cols = lax.broadcasted_iota(jnp.int32, (block, block), 1)
        return (rows == cols).astype(F32)

    def span(i):
        return slice(i * block, (i + 1) * block)

    def put_split(high_ref, low_ref, i, j, value):
        high, low = split(value)
        high_ref[span(i), span(j)], low_ref[span(i), span(j)] = high, low

    for i in range(NX):
        e[span(i), span(i)] = e[span(i), span(i)] - eye()
        far, spare = span((i + 2) % NX), span((i - 1) % NX)
        e[span(i), far] = e[span(i), far] + s[span(i), spare]
        start = eye() - n[span(i), span(i)]
        n[span(i), span(i)] = start
        put_split(xh, xl, i, i, 0.5 * start)
        put_split(sh, sl, i, i, s[span(i), span(i)])
        k = (i + 1) % NX
        put_split(sh, sl, i, k, s[span(i), span(k)])
        put_split(sh, sl, k, i, s[span(i), span(k)].T)
        for j in range(i):
            start = -(n[span(i), span(j)] + n[span(j), span(i)].T)
            n[span(i), span(j)] = start
            put_split(xh, xl, i, j, 0.5 * start)
            start = start.T
            n[span(j), span(i)] = start
            put_split(xh, xl, j, i, 0.5 * start)
            if i - j == 2:
                value = s[span(i), span(j)] + s[span(j), span(i)].T
                put_split(sh, sl, i, j, value)
                put_split(sh, sl, j, i, value.T)

    def columns(i):
        return pl.ds(pl.multiple_of(i * block, block), block)

    for sweep in range(ITERS - 2):

        def inner(i, carry):
            cols = columns(i)
            value = three((xh[...], xl[...]), (sh[:, cols], sl[:, cols]))
            high, low = split(-e[:, cols] - 0.5 * value)
            wh[:, cols], wl[:, cols] = high, low
            return carry

        lax.fori_loop(0, NX, inner, 0)

        def outer(i, carry):
            cols = columns(i)
            q[:total, cols] = three((wh[...], wl[...]), (xh[:, cols], xl[:, cols]))
            return carry

        lax.fori_loop(0, NX, outer, 0)
        for i in range(NX):
            for j in range(i + 1):
                value = 0.5 * (n[span(i), span(j)] + (q[span(i), span(j)] + q[span(j), span(i)].T))
                high, low = split(value)
                xh[span(i), span(j)], xl[span(i), span(j)] = high, low
                if i != j:
                    high, low = split(value.T)
                    xh[span(j), span(i)], xl[span(j), span(i)] = high, low

    row = (xh[:block], xl[:block])
    for j in range(NX):
        value = three(row, (sh[:, span(j)], sl[:, span(j)]))
        high, low = split(-e[:block, span(j)] - value)
        wh[:block, span(j)], wl[:block, span(j)] = high, low
    weight = (wh[:block], wl[:block])
    for j in range(NX):
        value = three(weight, (xh[:, span(j)], xl[:, span(j)]))
        value = value - three(row, split(e[span(j)]), dot_nt)
        q[:block, span(j)] = 0.5 * (n[:block, span(j)] + value)
    for j in range(NX):
        high, low = split(q[:block, span(j)])
        wh[:block, span(j)], wl[:block, span(j)] = high, low
        q[pl.ds(block + j * block, block), :block] = q[:block, span(j)].T
    begin = place[2]
    mult[...] = q[pl.ds(pl.multiple_of(block + begin, 16), mult.shape[0]), :block]
    value = trial[...]
    for j in range(NX):
        value = value + three((wh[:block, span(j)], wl[:block, span(j)]), split(olds[j][...]))
    c_new[...] = value


def local(c_old, c_trial):
    block, slab = c_old.shape
    total = block * NX
    x, y, z, core = (lax.axis_index(name) for name in ("x", "y", "z", "core"))
    grid_place = (z * NY + y) * NC + core
    tile_rows = total // (NZ * NY * NC)
    begin = (grid_place * tile_rows - x * block) % total
    place = jnp.stack([y, core, begin, x]).astype(jnp.int32)
    old_parts, tiles = gram(c_old, c_trial, place)
    tile = sum_over(sum_over(tiles, "y"), "z") * (1.0 / (slab * NC * NY * NZ))
    own, other = gather_all(tile)
    wide = pltpu.VMEM((total, total), F32)
    thin = pltpu.VMEM((total, total), BF16)
    count = 4 * PIECES + NX + 1
    return pl.pallas_call(
        functools.partial(constrain, block=block),
        out_shape=(
            jax.ShapeDtypeStruct((block, slab), F32),
            jax.ShapeDtypeStruct((tile_rows, block), F32),
        ),
        in_specs=[SMEM] + [VMEM] * count,
        out_specs=(VMEM, VMEM),
        scratch_shapes=[wide] * 3 + [thin] * 6 + [pltpu.VMEM((total + block, total), F32)],
        compiler_params=pltpu.CompilerParams(vmem_limit_bytes=VMEM_BYTES),
        cost_estimate=pl.CostEstimate(
            flops=40 * total**3, bytes_accessed=24 * 1024 * 1024, transcendentals=0
        ),
    )(place, *own, *other, *old_parts, c_trial)


def solution(mesh):
    fine = Mesh(mesh.devices.reshape(NZ, NY, NC, NX), ("z", "y", "core", "x"))
    grid = ("z", "y", "core")
    return jax.shard_map(
        local,
        mesh=fine,
        in_specs=(P("x", grid), P("x", grid)),
        out_specs=(P("x", grid), P(grid, "x")),
        check_vma=False,
    )
```

```python
import functools

import jax
import jax.numpy as jnp
from jax import lax
from jax.experimental import pallas as pl
from jax.experimental.pallas import tpu as pltpu
from jax.sharding import Mesh, PartitionSpec as P

ITERS = 4
NX, NY, NZ, NC = 4, 4, 8, 2
BF16, F32 = jnp.bfloat16, jnp.float32
PIECES = 5
SLOTS = 6
VMEM_BYTES = 56 * 1024 * 1024


def from_offset(value, axis, size, offset):
    return lax.ppermute(value, axis, [((i + offset) % size, i) for i in range(size)])


MESH_AXES = ("z", "y", "core", "x")


def along(value, turned, offset):
    pairs = []
    for z in range(NZ):
        for y in range(NY):
            for core in range(NC):
                for x in range(NX):
                    if (core == 0) != turned:
                        source = (z, (y + offset) % NY, core, x)
                    else:
                        source = (z, y, core, (x + offset) % NX)
                    places = (source, (z, y, core, x))
                    flat = [((a * NY + b) * NC + c) * NX + d for a, b, c, d in places]
                    pairs.append(tuple(flat))
    return lax.ppermute(value, MESH_AXES, pairs)


def ring_forward(value, turned):
    half = value.shape[0] // 2
    after = along(value, turned, 1)
    before = along(value, turned, -1)
    top = along(after[:half], turned, 1)
    low = along(before[half:], turned, -1)
    return [value, after, top, low, before]


def other_core(value):
    return from_offset(value, "core", NC, 1)


def split(value):
    high = value.astype(BF16)
    return high, (value - high.astype(F32)).astype(BF16)


def dot(left, right):
    return jnp.dot(left, right, preferred_element_type=F32)


def dot_nt(left, right):
    return lax.dot_general(left, right, (((1,), (1,)), ((), ())), preferred_element_type=F32)


def three(left, right, form=dot):
    return form(left[0], right[0]) + (form(left[0], right[1]) + form(left[1], right[0]))


def messages(place, trial, to_last, to_next):
    x = place[3]
    quarter = trial.shape[1] // NX
    for k, (ref, at) in enumerate(((to_last, 0), (to_last, 1), (to_next, 0), (to_next, 1))):
        ref[:, at * quarter : (at + 1) * quarter] = trial[:, quarter_at(x + k, quarter)]
    to_next[:, 2 * quarter :] = trial[:, quarter_at(x, quarter)]


def quarter_at(index, quarter):
    return pl.ds(pl.multiple_of(lax.rem(index, NX) * quarter, quarter), quarter)


def put_block(core, keep, send, slot, value):
    half = value.shape[0] // NC
    first = core == 0
    kept = jnp.where(first, value[:half], value[half:])
    sent = jnp.where(first, value[half:], value[:half])
    wide = value.shape[1] // 128
    deep = NZ // wide
    for y in range(NY):
        for z in range(NZ):
            rows = slice((y * deep + z // wide) * 8, (y * deep + z // wide) * 8 + 8)
            cols = slice(z % wide * 128, z % wide * 128 + 128)
            keep[y, z, slot] = kept[rows, cols]
            send[y, z, slot] = sent[rows, cols]


def near_blocks(place, trial, old, after, before, keep, send):
    core = place[1]
    t, c, a, b = (split(ref[...]) for ref in (trial, old, after, before))
    pairs = ((t, c), (t, a), (t, b), (c, c), (c, a), (t, t))
    for slot, (left, right) in enumerate(pairs):
        put_block(core, keep, send, slot, three(left, right, dot_nt))


def far_blocks(place, trial, trial_after, trial_before, after, before, keep, send):
    core, x = place[1], place[3]
    quarter = trial.shape[1] // NX

    def pair(ref, first):
        parts = [split(ref[:, quarter_at(x + first + k, quarter)]) for k in range(2)]
        return tuple(jnp.concatenate([parts[0][k], parts[1][k]], axis=1) for k in range(2))

    ta = split(trial_after[...])
    tb = split(trial_before[...])
    tb_first = tuple(part[:, : 2 * quarter] for part in tb)
    tb_second = tuple(part[:, quarter:] for part in tb)
    ca, cb = pair(after, 1), pair(before, 1)
    pairs = (
        (tb_first, ca),
        (ta, cb),
        (cb, ca),
        (tb_first, ta),
        (pair(trial, 1), ta),
        (pair(trial, 2), tb_second),
    )
    for slot, (left, right) in enumerate(pairs):
        put_block(core, keep, send, slot, three(left, right, dot_nt))


VMEM = pl.BlockSpec(memory_space=pltpu.VMEM)
SMEM = pl.BlockSpec(memory_space=pltpu.SMEM)


def tile_kernel(body, place, operands, block, flops):
    tiles = jax.ShapeDtypeStruct((NY, NZ, SLOTS, 8, 128), F32)
    keep, send = pl.pallas_call(
        body,
        out_shape=(tiles, tiles),
        in_specs=[SMEM] + [VMEM] * len(operands),
        out_specs=(VMEM, VMEM),
        compiler_params=pltpu.CompilerParams(vmem_limit_bytes=32 * 1024 * 1024),
        cost_estimate=pl.CostEstimate(
            flops=flops, bytes_accessed=6 * 1024 * 1024, transcendentals=0
        ),
    )(place, *operands)
    return keep, other_core(send)


def gram(c_old, c_trial, place):
    block, slab = c_old.shape
    quarter = slab // NX
    after = from_offset(c_old, "x", NX, 1)
    before = from_offset(c_old, "x", NX, -1)
    to_last, to_next = pl.pallas_call(
        messages,
        out_shape=(
            jax.ShapeDtypeStruct((block, 2 * quarter), F32),
            jax.ShapeDtypeStruct((block, 3 * quarter), F32),
        ),
        in_specs=[SMEM, VMEM],
        out_specs=(VMEM, VMEM),
    )(place, c_trial)
    trial_after = from_offset(to_last, "x", NX, 1)
    trial_before = from_offset(to_next, "x", NX, -1)
    flops = 6 * 6 * block * block * slab
    near, near_other = tile_kernel(
        near_blocks, place, (c_trial, c_old, after, before), block, flops
    )
    near, trial_after, trial_before = lax.optimization_barrier((near, trial_after, trial_before))
    far, far_other = tile_kernel(
        far_blocks, place, (c_trial, trial_after, trial_before, after, before), block, flops // 2
    )
    to_far, far = lax.optimization_barrier((c_old, far))
    far_old = from_offset(to_far, "x", NX, 2)
    tiles = jnp.concatenate([near + near_other, far + far_other], axis=2)
    return [c_old, after, far_old, before], tiles


def sum_over(tiles, axis):
    return jnp.sum(lax.all_to_all(tiles, axis, 0, 0), axis=0)


def gather_over_z(tile):
    return lax.all_to_all(jnp.broadcast_to(tile[None], (NZ,) + tile.shape), "z", 0, 0)


def gather_all(tile):
    tiles = gather_over_z(tile)
    core = lax.axis_index("core")
    half = NZ // NC
    mine = lax.dynamic_slice_in_dim(tiles, core * half, half, 0)
    give = lax.dynamic_slice_in_dim(tiles, (1 - core) * half, half, 0)
    pair = jnp.stack([mine, other_core(give)])
    around = jnp.stack([pair] + [along(pair, False, r) for r in range(1, NY)])
    pieces = ring_forward(around, True)
    return pieces, [other_core(part) for part in pieces]


def constrain(place, *refs, block):
    count = PIECES
    own, other = refs[:count], refs[count : 2 * count]
    olds = refs[2 * count : 2 * count + NX]
    trial, c_new, mult = refs[2 * count + NX : 2 * count + NX + 3]
    e, s, n, xh, xl, sh, sl, wh, wl, q = refs[2 * count + NX + 3 :]
    total = NX * block
    y, core = place[0], place[1]
    lanes = 128
    wide = block // lanes
    core_rows = block // NC
    y_rows = core_rows // NY

    def put(value, which, shift, turn, z):
        group = lax.rem(y + turn, NY)
        inside = which * core_rows + group * y_rows + z // wide * 8
        r, after, before = shift, (shift + 1) % NX, (shift - 1) % NX
        targets = (
            (e, r, r),
            (e, r, after),
            (e, r, before),
            (s, r, r),
            (s, r, after),
            (n, r, r),
            (e, before, after),
            (s, after, r),
            (s, before, after),
            (n, before, after),
            (n, r, after),
            (n, r, before),
        )
        for k, (ref, row, col) in enumerate(targets):
            column = col * block + z % wide * lanes
            row = pl.multiple_of(row * block + inside, 8)
            ref[pl.ds(row, 8), column : column + lanes] = value[k]

    def piece(parts, offset, index):
        if offset == 2:
            half = NX // 2
            return parts[2 + index // half], index % half
        return parts[offset if offset < 2 else offset + 1], index

    def assemble(me):
        for family, parts in enumerate((own, other) if me == 0 else (other, own)):
            for shift in range(NX):
                for turn in range(NY):
                    offset, at = (shift, turn) if family == 0 else (turn, shift)
                    ref, index = piece(parts, offset, at)
                    for which in range(NC):
                        for z in range(NZ // NC):
                            value = ref[index, which ^ family, z]
                            put(value, which, shift, turn, family * (NZ // NC) + z)

    for me in range(NC):
        pl.when(core == me)(functools.partial(assemble, me))

    def eye():
        rows = lax.broadcasted_iota(jnp.int32, (block, block), 0)
        cols = lax.broadcasted_iota(jnp.int32, (block, block), 1)
        return (rows == cols).astype(F32)

    def span(i):
        return slice(i * block, (i + 1) * block)

    def put_split(high_ref, low_ref, i, j, value):
        high, low = split(value)
        high_ref[span(i), span(j)], low_ref[span(i), span(j)] = high, low

    for i in range(NX):
        e[span(i), span(i)] = e[span(i), span(i)] - eye()
        far, spare = span((i + 2) % NX), span((i - 1) % NX)
        e[span(i), far] = e[span(i), far] + s[span(i), spare]
        start = eye() - n[span(i), span(i)]
        n[span(i), span(i)] = start
        put_split(xh, xl, i, i, 0.5 * start)
        put_split(sh, sl, i, i, s[span(i), span(i)])
        k = (i + 1) % NX
        put_split(sh, sl, i, k, s[span(i), span(k)])
        put_split(sh, sl, k, i, s[span(i), span(k)].T)
        for j in range(i):
            start = -(n[span(i), span(j)] + n[span(j), span(i)].T)
            n[span(i), span(j)] = start
            put_split(xh, xl, i, j, 0.5 * start)
            start = start.T
            n[span(j), span(i)] = start
            put_split(xh, xl, j, i, 0.5 * start)
            if i - j == 2:
                value = s[span(i), span(j)] + s[span(j), span(i)].T
                put_split(sh, sl, i, j, value)
                put_split(sh, sl, j, i, value.T)

    def columns(i):
        return pl.ds(pl.multiple_of(i * block, block), block)

    for sweep in range(ITERS - 2):

        def inner(i, carry):
            cols = columns(i)
            value = three((xh[...], xl[...]), (sh[:, cols], sl[:, cols]))
            high, low = split(-e[:, cols] - 0.5 * value)
            wh[:, cols], wl[:, cols] = high, low
            return carry

        lax.fori_loop(0, NX, inner, 0)

        def outer(i, carry):
            cols = columns(i)
            q[:total, cols] = three((wh[...], wl[...]), (xh[:, cols], xl[:, cols]))
            return carry

        lax.fori_loop(0, NX, outer, 0)
        for i in range(NX):
            for j in range(i + 1):
                value = 0.5 * (n[span(i), span(j)] + (q[span(i), span(j)] + q[span(j), span(i)].T))
                high, low = split(value)
                xh[span(i), span(j)], xl[span(i), span(j)] = high, low
                if i != j:
                    high, low = split(value.T)
                    xh[span(j), span(i)], xl[span(j), span(i)] = high, low

    row = (xh[:block], xl[:block])
    for j in range(NX):
        value = three(row, (sh[:, span(j)], sl[:, span(j)]))
        high, low = split(-e[:block, span(j)] - value)
        wh[:block, span(j)], wl[:block, span(j)] = high, low
    weight = (wh[:block], wl[:block])
    for j in range(NX):
        value = three(weight, (xh[:, span(j)], xl[:, span(j)]))
        value = value - three(row, split(e[span(j)]), dot_nt)
        q[:block, span(j)] = 0.5 * (n[:block, span(j)] + value)
    for j in range(NX):
        high, low = split(q[:block, span(j)])
        wh[:block, span(j)], wl[:block, span(j)] = high, low
        q[pl.ds(block + j * block, block), :block] = q[:block, span(j)].T
    begin = place[2]
    mult[...] = q[pl.ds(pl.multiple_of(block + begin, 16), mult.shape[0]), :block]
    value = trial[...]
    for j in range(NX):
        value = value + three((wh[:block, span(j)], wl[:block, span(j)]), split(olds[j][...]))
    c_new[...] = value


def local(c_old, c_trial):
    block, slab = c_old.shape
    total = block * NX
    x, y, z, core = (lax.axis_index(name) for name in ("x", "y", "z", "core"))
    grid_place = (z * NY + y) * NC + core
    tile_rows = total // (NZ * NY * NC)
    begin = (grid_place * tile_rows - x * block) % total
    place = jnp.stack([y, core, begin, x]).astype(jnp.int32)
    old_parts, tiles = gram(c_old, c_trial, place)
    tiles = sum_over(tiles, "y")
    tiles, old_parts[2] = lax.optimization_barrier((tiles, old_parts[2]))
    tile = sum_over(tiles, "z") * (1.0 / (slab * NC * NY * NZ))
    own, other = gather_all(tile)
    wide = pltpu.VMEM((total, total), F32)
    thin = pltpu.VMEM((total, total), BF16)
    count = 2 * PIECES + NX + 1
    return pl.pallas_call(
        functools.partial(constrain, block=block),
        out_shape=(
            jax.ShapeDtypeStruct((block, slab), F32),
            jax.ShapeDtypeStruct((tile_rows, block), F32),
        ),
        in_specs=[SMEM] + [VMEM] * count,
        out_specs=(VMEM, VMEM),
        scratch_shapes=[wide] * 3 + [thin] * 6 + [pltpu.VMEM((total + block, total), F32)],
        compiler_params=pltpu.CompilerParams(vmem_limit_bytes=VMEM_BYTES),
        cost_estimate=pl.CostEstimate(
            flops=40 * total**3, bytes_accessed=24 * 1024 * 1024, transcendentals=0
        ),
    )(place, *own, *other, *old_parts, c_trial)


def solution(mesh):
    fine = Mesh(mesh.devices.reshape(NZ, NY, NC, NX), ("z", "y", "core", "x"))
    grid = ("z", "y", "core")
    return jax.shard_map(
        local,
        mesh=fine,
        in_specs=(P("x", grid), P("x", grid)),
        out_specs=(P("x", grid), P(grid, "x")),
        check_vma=False,
    )
```

```python
import functools

import jax
import jax.numpy as jnp
from jax import lax
from jax.experimental import pallas as pl
from jax.experimental.pallas import tpu as pltpu
from jax.sharding import Mesh, PartitionSpec as P

ITERS = 4
NX, NY, NZ, NC = 4, 4, 8, 2
BF16, F32 = jnp.bfloat16, jnp.float32
PIECES = 8
SLOTS = 6
VMEM_BYTES = 43 * 1024 * 1024


def from_offset(value, axis, size, offset):
    return lax.ppermute(value, axis, [((i + offset) % size, i) for i in range(size)])


MESH_AXES = ("z", "y", "core", "x")


def along(value, turned, offset):
    pairs = []
    for z in range(NZ):
        for y in range(NY):
            for core in range(NC):
                for x in range(NX):
                    if (core == 0) != turned:
                        source = (z, (y + offset) % NY, core, x)
                    else:
                        source = (z, y, core, (x + offset) % NX)
                    places = (source, (z, y, core, x))
                    flat = [((a * NY + b) * NC + c) * NX + d for a, b, c, d in places]
                    pairs.append(tuple(flat))
    return lax.ppermute(value, MESH_AXES, pairs)


def ring_forward(top, low, turned):
    after_top = along(top, turned, 1)
    before_low = along(low, turned, -1)
    after_low = along(low, turned, 1)
    before_top = along(top, turned, -1)
    far_top = along(after_top, turned, 1)
    far_low = along(before_low, turned, -1)
    return [top, low, after_top, after_low, far_top, far_low, before_top, before_low]


def other_core(value):
    return from_offset(value, "core", NC, 1)


def split(value):
    high = value.astype(BF16)
    return high, (value - high.astype(F32)).astype(BF16)


def dot(left, right):
    return jnp.dot(left, right, preferred_element_type=F32)


def dot_nt(left, right):
    return lax.dot_general(left, right, (((1,), (1,)), ((), ())), preferred_element_type=F32)


def three(left, right, form=dot):
    return form(left[0], right[0]) + (form(left[0], right[1]) + form(left[1], right[0]))


def messages(place, trial, to_last, to_next):
    x = place[3]
    quarter = trial.shape[1] // NX
    for k, (ref, at) in enumerate(((to_last, 0), (to_last, 1), (to_next, 0), (to_next, 1))):
        ref[:, at * quarter : (at + 1) * quarter] = trial[:, quarter_at(x + k, quarter)]
    to_next[:, 2 * quarter :] = trial[:, quarter_at(x, quarter)]


def quarter_at(index, quarter):
    return pl.ds(pl.multiple_of(lax.rem(index, NX) * quarter, quarter), quarter)


def put_block(core, keep, send, slot, value):
    half = value.shape[0] // NC
    first = core == 0
    kept = jnp.where(first, value[:half], value[half:])
    sent = jnp.where(first, value[half:], value[:half])
    wide = value.shape[1] // 128
    deep = NZ // wide
    for y in range(NY):
        for z in range(NZ):
            rows = slice((y * deep + z // wide) * 8, (y * deep + z // wide) * 8 + 8)
            cols = slice(z % wide * 128, z % wide * 128 + 128)
            keep[y, z, slot] = kept[rows, cols]
            send[y, z, slot] = sent[rows, cols]


def near_blocks(place, trial, old, after, before, keep, send):
    core = place[1]
    t, c, a, b = (split(ref[...]) for ref in (trial, old, after, before))
    pairs = ((t, c), (t, a), (t, b), (c, c), (c, a), (t, t))
    for slot, (left, right) in enumerate(pairs):
        put_block(core, keep, send, slot, three(left, right, dot_nt))


def far_blocks(place, trial, trial_after, trial_before, after, before, keep, send):
    core, x = place[1], place[3]
    quarter = trial.shape[1] // NX

    def pair(ref, first):
        parts = [split(ref[:, quarter_at(x + first + k, quarter)]) for k in range(2)]
        return tuple(jnp.concatenate([parts[0][k], parts[1][k]], axis=1) for k in range(2))

    ta = split(trial_after[...])
    tb = split(trial_before[...])
    tb_first = tuple(part[:, : 2 * quarter] for part in tb)
    tb_second = tuple(part[:, quarter:] for part in tb)
    ca, cb = pair(after, 1), pair(before, 1)
    pairs = (
        (tb_first, ca),
        (ta, cb),
        (cb, ca),
        (tb_first, ta),
        (pair(trial, 1), ta),
        (pair(trial, 2), tb_second),
    )
    for slot, (left, right) in enumerate(pairs):
        put_block(core, keep, send, slot, three(left, right, dot_nt))


VMEM = pl.BlockSpec(memory_space=pltpu.VMEM)
SMEM = pl.BlockSpec(memory_space=pltpu.SMEM)


def tile_kernel(body, place, operands, block, flops):
    tiles = jax.ShapeDtypeStruct((NY, NZ, SLOTS, 8, 128), F32)
    keep, send = pl.pallas_call(
        body,
        out_shape=(tiles, tiles),
        in_specs=[SMEM] + [VMEM] * len(operands),
        out_specs=(VMEM, VMEM),
        compiler_params=pltpu.CompilerParams(vmem_limit_bytes=32 * 1024 * 1024),
        cost_estimate=pl.CostEstimate(
            flops=flops, bytes_accessed=6 * 1024 * 1024, transcendentals=0
        ),
    )(place, *operands)
    return keep, other_core(send)


def gram(c_old, c_trial, place):
    block, slab = c_old.shape
    quarter = slab // NX
    after = from_offset(c_old, "x", NX, 1)
    before = from_offset(c_old, "x", NX, -1)
    to_last, to_next = pl.pallas_call(
        messages,
        out_shape=(
            jax.ShapeDtypeStruct((block, 2 * quarter), F32),
            jax.ShapeDtypeStruct((block, 3 * quarter), F32),
        ),
        in_specs=[SMEM, VMEM],
        out_specs=(VMEM, VMEM),
    )(place, c_trial)
    trial_after = from_offset(to_last, "x", NX, 1)
    trial_before = from_offset(to_next, "x", NX, -1)
    flops = 6 * 6 * block * block * slab
    near, near_other = tile_kernel(
        near_blocks, place, (c_trial, c_old, after, before), block, flops
    )
    near, trial_after, trial_before = lax.optimization_barrier((near, trial_after, trial_before))
    far, far_other = tile_kernel(
        far_blocks, place, (c_trial, trial_after, trial_before, after, before), block, flops // 2
    )
    to_far, far = lax.optimization_barrier((c_old, far))
    far_old = from_offset(to_far, "x", NX, 2)
    tiles = jnp.concatenate([near + near_other, far + far_other], axis=2)
    return [c_old, after, far_old, before], tiles


def sum_over(tiles, axis):
    return jnp.sum(lax.all_to_all(tiles, axis, 0, 0), axis=0)


def gather_over_z(tile):
    return lax.all_to_all(jnp.broadcast_to(tile[None], (NZ,) + tile.shape), "z", 0, 0)


def gather_all(tile):
    mine = gather_over_z(tile)
    parts = [mine] + [along(mine, False, r) for r in range(1, NY)]
    pieces = ring_forward(jnp.stack(parts[:2]), jnp.stack(parts[2:]), True)
    return pieces, [other_core(part) for part in pieces]


def constrain(place, *refs, block):
    count = PIECES
    own, other = refs[:count], refs[count : 2 * count]
    olds = refs[2 * count : 2 * count + NX]
    trial, c_new, mult = refs[2 * count + NX : 2 * count + NX + 3]
    e, s, n, xh, xl, sh, sl, wh, wl, q = refs[2 * count + NX + 3 :]
    total = NX * block
    y, core = place[0], place[1]
    lanes = 128
    wide = block // lanes
    core_rows = block // NC
    y_rows = core_rows // NY

    def put(value, which, shift, turn, z):
        group = lax.rem(y + turn, NY)
        inside = which * core_rows + group * y_rows + z // wide * 8
        r, after, before = shift, (shift + 1) % NX, (shift - 1) % NX
        targets = (
            (e, r, r),
            (e, r, after),
            (e, r, before),
            (s, r, r),
            (s, r, after),
            (n, r, r),
            (e, before, after),
            (s, after, r),
            (s, before, after),
            (n, before, after),
            (n, r, after),
            (n, r, before),
        )
        for k, (ref, row, col) in enumerate(targets):
            column = col * block + z % wide * lanes
            row = pl.multiple_of(row * block + inside, 8)
            ref[pl.ds(row, 8), column : column + lanes] = value[k]

    def assemble(me):
        for which, parts in enumerate((own, other) if me == 0 else (other, own)):
            for shift in range(NX):
                for turn in range(NY):
                    offset, at = (shift, turn) if which == 0 else (turn, shift)
                    for z in range(NZ):
                        value = parts[2 * offset + at // 2][at % 2, z]
                        put(value, which, shift, turn, z)

    for me in range(NC):
        pl.when(core == me)(functools.partial(assemble, me))

    def eye():
        rows = lax.broadcasted_iota(jnp.int32, (block, block), 0)
        cols = lax.broadcasted_iota(jnp.int32, (block, block), 1)
        return (rows == cols).astype(F32)

    def span(i):
        return slice(i * block, (i + 1) * block)

    def put_split(high_ref, low_ref, i, j, value):
        high, low = split(value)
        high_ref[span(i), span(j)], low_ref[span(i), span(j)] = high, low

    for i in range(NX):
        e[span(i), span(i)] = e[span(i), span(i)] - eye()
        far, spare = span((i + 2) % NX), span((i - 1) % NX)
        e[span(i), far] = e[span(i), far] + s[span(i), spare]
        start = eye() - n[span(i), span(i)]
        n[span(i), span(i)] = start
        put_split(xh, xl, i, i, 0.5 * start)
        put_split(sh, sl, i, i, s[span(i), span(i)])
        k = (i + 1) % NX
        put_split(sh, sl, i, k, s[span(i), span(k)])
        put_split(sh, sl, k, i, s[span(i), span(k)].T)
        for j in range(i):
            start = -(n[span(i), span(j)] + n[span(j), span(i)].T)
            n[span(i), span(j)] = start
            put_split(xh, xl, i, j, 0.5 * start)
            start = start.T
            n[span(j), span(i)] = start
            put_split(xh, xl, j, i, 0.5 * start)
            if i - j == 2:
                value = s[span(i), span(j)] + s[span(j), span(i)].T
                put_split(sh, sl, i, j, value)
                put_split(sh, sl, j, i, value.T)

    def columns(i):
        return pl.ds(pl.multiple_of(i * block, block), block)

    for sweep in range(ITERS - 2):

        def inner(i, carry):
            cols = columns(i)
            value = three((xh[...], xl[...]), (sh[:, cols], sl[:, cols]))
            high, low = split(-e[:, cols] - 0.5 * value)
            wh[:, cols], wl[:, cols] = high, low
            return carry

        lax.fori_loop(0, NX, inner, 0)

        def outer(i, carry):
            cols = columns(i)
            q[:total, cols] = three((wh[...], wl[...]), (xh[:, cols], xl[:, cols]))
            return carry

        lax.fori_loop(0, NX, outer, 0)
        for i in range(NX):
            for j in range(i + 1):
                value = 0.5 * (n[span(i), span(j)] + (q[span(i), span(j)] + q[span(j), span(i)].T))
                high, low = split(value)
                xh[span(i), span(j)], xl[span(i), span(j)] = high, low
                if i != j:
                    high, low = split(value.T)
                    xh[span(j), span(i)], xl[span(j), span(i)] = high, low

    row = (xh[:block], xl[:block])
    for j in range(NX):
        value = three(row, (sh[:, span(j)], sl[:, span(j)]))
        high, low = split(-e[:block, span(j)] - value)
        wh[:block, span(j)], wl[:block, span(j)] = high, low
    weight = (wh[:block], wl[:block])
    for j in range(NX):
        value = three(weight, (xh[:, span(j)], xl[:, span(j)]))
        value = value - three(row, split(e[span(j)]), dot_nt)
        q[:block, span(j)] = 0.5 * (n[:block, span(j)] + value)
    for j in range(NX):
        high, low = split(q[:block, span(j)])
        wh[:block, span(j)], wl[:block, span(j)] = high, low
        q[pl.ds(block + j * block, block), :block] = q[:block, span(j)].T
    begin = place[2]
    mult[...] = q[pl.ds(pl.multiple_of(block + begin, 16), mult.shape[0]), :block]
    value = trial[...]
    for j in range(NX):
        value = value + three((wh[:block, span(j)], wl[:block, span(j)]), split(olds[j][...]))
    c_new[...] = value


def local(c_old, c_trial):
    block, slab = c_old.shape
    total = block * NX
    x, y, z, core = (lax.axis_index(name) for name in ("x", "y", "z", "core"))
    grid_place = (z * NY + y) * NC + core
    tile_rows = total // (NZ * NY * NC)
    begin = (grid_place * tile_rows - x * block) % total
    place = jnp.stack([y, core, begin, x]).astype(jnp.int32)
    old_parts, tiles = gram(c_old, c_trial, place)
    tiles = sum_over(tiles, "y")
    tile = sum_over(tiles, "z") * (1.0 / (slab * NC * NY * NZ))
    tile, old_parts[2] = lax.optimization_barrier((tile, old_parts[2]))
    own, other = gather_all(tile)
    wide = pltpu.VMEM((total, total), F32)
    thin = pltpu.VMEM((total, total), BF16)
    count = 2 * PIECES + NX + 1
    return pl.pallas_call(
        functools.partial(constrain, block=block),
        out_shape=(
            jax.ShapeDtypeStruct((block, slab), F32),
            jax.ShapeDtypeStruct((tile_rows, block), F32),
        ),
        in_specs=[SMEM] + [VMEM] * count,
        out_specs=(VMEM, VMEM),
        scratch_shapes=[wide] * 3 + [thin] * 6 + [pltpu.VMEM((total + block, total), F32)],
        compiler_params=pltpu.CompilerParams(vmem_limit_bytes=VMEM_BYTES),
        cost_estimate=pl.CostEstimate(
            flops=40 * total**3, bytes_accessed=24 * 1024 * 1024, transcendentals=0
        ),
    )(place, *own, *other, *old_parts, c_trial)


def solution(mesh):
    fine = Mesh(mesh.devices.reshape(NZ, NY, NC, NX), ("z", "y", "core", "x"))
    grid = ("z", "y", "core")
    return jax.shard_map(
        local,
        mesh=fine,
        in_specs=(P("x", grid), P("x", grid)),
        out_specs=(P("x", grid), P(grid, "x")),
        check_vma=False,
    )
```

```python
import functools

import jax
import jax.numpy as jnp
from jax import lax
from jax.experimental import pallas as pl
from jax.experimental.pallas import tpu as pltpu
from jax.sharding import Mesh, PartitionSpec as P

ITERS = 4
NX, NY, NZ, NC = 4, 4, 8, 2
BF16, F32 = jnp.bfloat16, jnp.float32
PIECES = 8
SLOTS = 6
VMEM_BYTES = 43 * 1024 * 1024


def from_offset(value, axis, size, offset):
    return lax.ppermute(value, axis, [((i + offset) % size, i) for i in range(size)])


MESH_AXES = ("z", "y", "core", "x")


def along(value, turned, offset):
    def source_of(z, y, core, x):
        if (core == 0) != turned:
            return z, (y + offset) % NY, core, x
        return z, y, core, (x + offset) % NX

    return from_source(value, source_of)


def mirrored(value, offset):
    def source_of(z, y, core, x):
        return z, y, core, (x + (offset if core == 0 else -offset)) % NX

    return from_source(value, source_of)


def from_source(value, source_of):
    pairs = []
    for z in range(NZ):
        for y in range(NY):
            for core in range(NC):
                for x in range(NX):
                    source = source_of(z, y, core, x)
                    places = (source, (z, y, core, x))
                    flat = [((a * NY + b) * NC + c) * NX + d for a, b, c, d in places]
                    pairs.append(tuple(flat))
    return lax.ppermute(value, MESH_AXES, pairs)


def ring_forward(top, low, turned):
    after_top = along(top, turned, 1)
    before_low = along(low, turned, -1)
    after_low = along(low, turned, 1)
    before_top = along(top, turned, -1)
    far_top = along(after_top, turned, 1)
    far_low = along(before_low, turned, -1)
    return [top, low, after_top, after_low, far_top, far_low, before_top, before_low]


def other_core(value):
    return from_offset(value, "core", NC, 1)


def split(value):
    high = value.astype(BF16)
    return high, (value - high.astype(F32)).astype(BF16)


def dot(left, right):
    return jnp.dot(left, right, preferred_element_type=F32)


def dot_nt(left, right):
    return lax.dot_general(left, right, (((1,), (1,)), ((), ())), preferred_element_type=F32)


def three(left, right, form=dot):
    return form(left[0], right[0]) + (form(left[0], right[1]) + form(left[1], right[0]))


def messages(place, trial, large, small):
    core, x = place[1], place[3]
    quarter = trial.shape[1] // NX
    first = x + 2 - 2 * core
    second = x + 3 * core
    for ref, begin, count in ((large, first, 3), (small, second, 2)):
        for k in range(count):
            ref[:, k * quarter : (k + 1) * quarter] = trial[:, quarter_at(begin + k, quarter)]


def quarter_at(index, quarter):
    return pl.ds(pl.multiple_of(lax.rem(index, NX) * quarter, quarter), quarter)


def put_block(core, keep, send, slot, value):
    half = value.shape[0] // NC
    first = core == 0
    kept = jnp.where(first, value[:half], value[half:])
    sent = jnp.where(first, value[half:], value[:half])
    wide = value.shape[1] // 128
    deep = NZ // wide
    for y in range(NY):
        for z in range(NZ):
            rows = slice((y * deep + z // wide) * 8, (y * deep + z // wide) * 8 + 8)
            cols = slice(z % wide * 128, z % wide * 128 + 128)
            keep[y, z, slot] = kept[rows, cols]
            send[y, z, slot] = sent[rows, cols]


def near_blocks(place, trial, old, after, before, keep, send):
    core = place[1]
    t, c, a, b = (split(ref[...]) for ref in (trial, old, after, before))
    pairs = ((t, c), (t, a), (t, b), (c, c), (c, a), (t, t))
    for slot, (left, right) in enumerate(pairs):
        put_block(core, keep, send, slot, three(left, right, dot_nt))


def far_blocks(place, trial, large, small, after, before, keep, send):
    core, x = place[1], place[3]
    quarter = trial.shape[1] // NX

    def pair(ref, first):
        parts = [split(ref[:, quarter_at(x + first + k, quarter)]) for k in range(2)]
        return tuple(jnp.concatenate([parts[0][k], parts[1][k]], axis=1) for k in range(2))

    def products(me):
        big, little = split(large[...]), split(small[...])
        big_first = tuple(part[:, : 2 * quarter] for part in big)
        big_second = tuple(part[:, quarter:] for part in big)
        if me == 0:
            ta, tb, ta_cross, tb_cross, cross = little, big_second, little, big_first, 1
        else:
            ta, tb, ta_cross, tb_cross, cross = big_first, little, big_second, little, 2
        ca, cb = pair(after, cross), pair(before, cross)
        pairs = (
            (tb_cross, ca),
            (ta_cross, cb),
            (cb, ca),
            (tb_cross, ta_cross),
            (pair(trial, 1), ta),
            (pair(trial, 2), tb),
        )
        for slot, (left, right) in enumerate(pairs):
            put_block(core, keep, send, slot, three(left, right, dot_nt))

    for me in range(NC):
        pl.when(core == me)(functools.partial(products, me))


VMEM = pl.BlockSpec(memory_space=pltpu.VMEM)
SMEM = pl.BlockSpec(memory_space=pltpu.SMEM)


def tile_kernel(body, place, operands, block, flops):
    tiles = jax.ShapeDtypeStruct((NY, NZ, SLOTS, 8, 128), F32)
    keep, send = pl.pallas_call(
        body,
        out_shape=(tiles, tiles),
        in_specs=[SMEM] + [VMEM] * len(operands),
        out_specs=(VMEM, VMEM),
        compiler_params=pltpu.CompilerParams(vmem_limit_bytes=32 * 1024 * 1024),
        cost_estimate=pl.CostEstimate(
            flops=flops, bytes_accessed=6 * 1024 * 1024, transcendentals=0
        ),
    )(place, *operands)
    return keep, other_core(send)


def gram(c_old, c_trial, place):
    block, slab = c_old.shape
    quarter = slab // NX
    after = from_offset(c_old, "x", NX, 1)
    before = from_offset(c_old, "x", NX, -1)
    large, small = pl.pallas_call(
        messages,
        out_shape=(
            jax.ShapeDtypeStruct((block, 3 * quarter), F32),
            jax.ShapeDtypeStruct((block, 2 * quarter), F32),
        ),
        in_specs=[SMEM, VMEM],
        out_specs=(VMEM, VMEM),
    )(place, c_trial)
    large = mirrored(large, -1)
    small = mirrored(small, 1)
    flops = 6 * 6 * block * block * slab
    near, near_other = tile_kernel(
        near_blocks, place, (c_trial, c_old, after, before), block, flops
    )
    near, large, small = lax.optimization_barrier((near + near_other, large, small))
    near = sum_over_y(near)
    far, far_other = tile_kernel(
        far_blocks, place, (c_trial, large, small, after, before), block, flops // 2
    )
    to_far, far = lax.optimization_barrier((c_old, far))
    far_old = from_offset(to_far, "x", NX, 2)
    far = sum_over_y(far + far_other)
    return [c_old, after, far_old, before], jnp.concatenate([near, far], axis=1)


def sum_over_y(tiles):
    y = lax.axis_index("y")
    total = lax.dynamic_index_in_dim(tiles, y, 0, keepdims=False)
    for offset in range(1, NY):
        part = lax.dynamic_index_in_dim(tiles, (y + offset) % NY, 0, keepdims=False)
        total = total + from_offset(part, "y", NY, -offset)
    return total


def sum_over_z(tiles):
    return jnp.sum(lax.all_to_all(tiles, "z", 0, 0), axis=0)


def gather_over_z(tile):
    return lax.all_to_all(jnp.broadcast_to(tile[None], (NZ,) + tile.shape), "z", 0, 0)


def gather_all(tile):
    mine = gather_over_z(tile)
    parts = [mine] + [along(mine, False, r) for r in range(1, NY)]
    pieces = ring_forward(jnp.stack(parts[:2]), jnp.stack(parts[2:]), True)
    return pieces, [other_core(part) for part in pieces]


def constrain(place, *refs, block):
    count = PIECES
    own, other = refs[:count], refs[count : 2 * count]
    olds = refs[2 * count : 2 * count + NX]
    trial, c_new, mult = refs[2 * count + NX : 2 * count + NX + 3]
    e, s, n, xh, xl, sh, sl, wh, wl, q = refs[2 * count + NX + 3 :]
    total = NX * block
    y, core = place[0], place[1]
    lanes = 128
    wide = block // lanes
    core_rows = block // NC
    y_rows = core_rows // NY

    def put(value, which, shift, turn, z):
        group = lax.rem(y + turn, NY)
        inside = which * core_rows + group * y_rows + z // wide * 8
        r, after, before = shift, (shift + 1) % NX, (shift - 1) % NX
        targets = (
            (e, r, r),
            (e, r, after),
            (e, r, before),
            (s, r, r),
            (s, r, after),
            (n, r, r),
            (e, before, after),
            (s, after, r),
            (s, before, after),
            (n, before, after),
            (n, r, after),
            (n, r, before),
        )
        for k, (ref, row, col) in enumerate(targets):
            column = col * block + z % wide * lanes
            row = pl.multiple_of(row * block + inside, 8)
            ref[pl.ds(row, 8), column : column + lanes] = value[k]

    def assemble(me):
        for which, parts in enumerate((own, other) if me == 0 else (other, own)):
            for shift in range(NX):
                for turn in range(NY):
                    offset, at = (shift, turn) if which == 0 else (turn, shift)
                    for z in range(NZ):
                        value = parts[2 * offset + at // 2][at % 2, z]
                        put(value, which, shift, turn, z)

    for me in range(NC):
        pl.when(core == me)(functools.partial(assemble, me))

    def eye():
        rows = lax.broadcasted_iota(jnp.int32, (block, block), 0)
        cols = lax.broadcasted_iota(jnp.int32, (block, block), 1)
        return (rows == cols).astype(F32)

    def span(i):
        return slice(i * block, (i + 1) * block)

    def put_split(high_ref, low_ref, i, j, value):
        high, low = split(value)
        high_ref[span(i), span(j)], low_ref[span(i), span(j)] = high, low

    for i in range(NX):
        e[span(i), span(i)] = e[span(i), span(i)] - eye()
        far, spare = span((i + 2) % NX), span((i - 1) % NX)
        e[span(i), far] = e[span(i), far] + s[span(i), spare]
        start = eye() - n[span(i), span(i)]
        n[span(i), span(i)] = start
        put_split(xh, xl, i, i, 0.5 * start)
        put_split(sh, sl, i, i, s[span(i), span(i)])
        k = (i + 1) % NX
        put_split(sh, sl, i, k, s[span(i), span(k)])
        put_split(sh, sl, k, i, s[span(i), span(k)].T)
        for j in range(i):
            start = -(n[span(i), span(j)] + n[span(j), span(i)].T)
            n[span(i), span(j)] = start
            put_split(xh, xl, i, j, 0.5 * start)
            start = start.T
            n[span(j), span(i)] = start
            put_split(xh, xl, j, i, 0.5 * start)
            if i - j == 2:
                value = s[span(i), span(j)] + s[span(j), span(i)].T
                put_split(sh, sl, i, j, value)
                put_split(sh, sl, j, i, value.T)

    def columns(i):
        return pl.ds(pl.multiple_of(i * block, block), block)

    for sweep in range(ITERS - 2):

        def inner(i, carry):
            cols = columns(i)
            value = three((xh[...], xl[...]), (sh[:, cols], sl[:, cols]))
            high, low = split(-e[:, cols] - 0.5 * value)
            wh[:, cols], wl[:, cols] = high, low
            return carry

        lax.fori_loop(0, NX, inner, 0)

        def outer(i, carry):
            cols = columns(i)
            q[:total, cols] = three((wh[...], wl[...]), (xh[:, cols], xl[:, cols]))
            return carry

        lax.fori_loop(0, NX, outer, 0)
        for i in range(NX):
            for j in range(i + 1):
                value = 0.5 * (n[span(i), span(j)] + (q[span(i), span(j)] + q[span(j), span(i)].T))
                high, low = split(value)
                xh[span(i), span(j)], xl[span(i), span(j)] = high, low
                if i != j:
                    high, low = split(value.T)
                    xh[span(j), span(i)], xl[span(j), span(i)] = high, low

    row = (xh[:block], xl[:block])
    for j in range(NX):
        value = three(row, (sh[:, span(j)], sl[:, span(j)]))
        high, low = split(-e[:block, span(j)] - value)
        wh[:block, span(j)], wl[:block, span(j)] = high, low
    weight = (wh[:block], wl[:block])
    for j in range(NX):
        value = three(weight, (xh[:, span(j)], xl[:, span(j)]))
        value = value - three(row, split(e[span(j)]), dot_nt)
        q[:block, span(j)] = 0.5 * (n[:block, span(j)] + value)
    for j in range(NX):
        high, low = split(q[:block, span(j)])
        wh[:block, span(j)], wl[:block, span(j)] = high, low
        q[pl.ds(block + j * block, block), :block] = q[:block, span(j)].T
    begin = place[2]
    mult[...] = q[pl.ds(pl.multiple_of(block + begin, 16), mult.shape[0]), :block]
    value = trial[...]
    for j in range(NX):
        value = value + three((wh[:block, span(j)], wl[:block, span(j)]), split(olds[j][...]))
    c_new[...] = value


def local(c_old, c_trial):
    block, slab = c_old.shape
    total = block * NX
    x, y, z, core = (lax.axis_index(name) for name in ("x", "y", "z", "core"))
    grid_place = (z * NY + y) * NC + core
    tile_rows = total // (NZ * NY * NC)
    begin = (grid_place * tile_rows - x * block) % total
    place = jnp.stack([y, core, begin, x]).astype(jnp.int32)
    old_parts, tiles = gram(c_old, c_trial, place)
    tile = sum_over_z(tiles) * (1.0 / (slab * NC * NY * NZ))
    tile, old_parts[2] = lax.optimization_barrier((tile, old_parts[2]))
    own, other = gather_all(tile)
    wide = pltpu.VMEM((total, total), F32)
    thin = pltpu.VMEM((total, total), BF16)
    count = 2 * PIECES + NX + 1
    return pl.pallas_call(
        functools.partial(constrain, block=block),
        out_shape=(
            jax.ShapeDtypeStruct((block, slab), F32),
            jax.ShapeDtypeStruct((tile_rows, block), F32),
        ),
        in_specs=[SMEM] + [VMEM] * count,
        out_specs=(VMEM, VMEM),
        scratch_shapes=[wide] * 3 + [thin] * 6 + [pltpu.VMEM((total + block, total), F32)],
        compiler_params=pltpu.CompilerParams(vmem_limit_bytes=VMEM_BYTES),
        cost_estimate=pl.CostEstimate(
            flops=40 * total**3, bytes_accessed=24 * 1024 * 1024, transcendentals=0
        ),
    )(place, *own, *other, *old_parts, c_trial)


def solution(mesh):
    fine = Mesh(mesh.devices.reshape(NZ, NY, NC, NX), ("z", "y", "core", "x"))
    grid = ("z", "y", "core")
    return jax.shard_map(
        local,
        mesh=fine,
        in_specs=(P("x", grid), P("x", grid)),
        out_specs=(P("x", grid), P(grid, "x")),
        check_vma=False,
    )
```

```python
import functools

import jax
import jax.numpy as jnp
from jax import lax
from jax.experimental import pallas as pl
from jax.experimental.pallas import tpu as pltpu
from jax.sharding import Mesh, PartitionSpec as P

ITERS = 4
NX, NY, NZ, NC = 4, 4, 8, 2
BF16, F32 = jnp.bfloat16, jnp.float32
PIECES = 8
SLOTS = 6
VMEM_BYTES = 43 * 1024 * 1024


def from_offset(value, axis, size, offset):
    return lax.ppermute(value, axis, [((i + offset) % size, i) for i in range(size)])


MESH_AXES = ("z", "y", "core", "x")


def along(value, turned, offset):
    def source_of(z, y, core, x):
        if (core == 0) != turned:
            return z, (y + offset) % NY, core, x
        return z, y, core, (x + offset) % NX

    return from_source(value, source_of)


def mirrored(value, offset):
    def source_of(z, y, core, x):
        return z, y, core, (x + (offset if core == 0 else -offset)) % NX

    return from_source(value, source_of)


def from_source(value, source_of):
    pairs = []
    for z in range(NZ):
        for y in range(NY):
            for core in range(NC):
                for x in range(NX):
                    source = source_of(z, y, core, x)
                    places = (source, (z, y, core, x))
                    flat = [((a * NY + b) * NC + c) * NX + d for a, b, c, d in places]
                    pairs.append(tuple(flat))
    return lax.ppermute(value, MESH_AXES, pairs)


def ring_forward(top, low, turned):
    after_top = along(top, turned, 1)
    before_low = along(low, turned, -1)
    after_low = along(low, turned, 1)
    before_top = along(top, turned, -1)
    far_top = along(after_top, turned, 1)
    far_low = along(before_low, turned, -1)
    return [top, low, after_top, after_low, far_top, far_low, before_top, before_low]


def other_core(value):
    return from_offset(value, "core", NC, 1)


def split(value):
    high = value.astype(BF16)
    return high, (value - high.astype(F32)).astype(BF16)


def dot(left, right):
    return jnp.dot(left, right, preferred_element_type=F32)


def dot_nt(left, right):
    return lax.dot_general(left, right, (((1,), (1,)), ((), ())), preferred_element_type=F32)


def three(left, right, form=dot):
    return form(left[0], right[0]) + (form(left[0], right[1]) + form(left[1], right[0]))


def messages(place, trial, large, small):
    core, x = place[1], place[3]
    quarter = trial.shape[1] // NX
    first = x + 2 - 2 * core
    second = x + 3 * core
    for ref, begin, count in ((large, first, 3), (small, second, 2)):
        for k in range(count):
            ref[:, k * quarter : (k + 1) * quarter] = trial[:, quarter_at(begin + k, quarter)]


def quarter_at(index, quarter):
    return pl.ds(pl.multiple_of(lax.rem(index, NX) * quarter, quarter), quarter)


def put_block(core, keep, send, slot, value):
    half = value.shape[0] // NC
    first = core == 0
    kept = jnp.where(first, value[:half], value[half:])
    sent = jnp.where(first, value[half:], value[:half])
    wide = value.shape[1] // 128
    deep = NZ // wide
    for y in range(NY):
        for z in range(NZ):
            rows = slice((y * deep + z // wide) * 8, (y * deep + z // wide) * 8 + 8)
            cols = slice(z % wide * 128, z % wide * 128 + 128)
            keep[y, z, slot] = kept[rows, cols]
            send[y, z, slot] = sent[rows, cols]


def near_blocks(place, trial, old, after, before, keep, send):
    core = place[1]
    t, c, a, b = (split(ref[...]) for ref in (trial, old, after, before))
    pairs = ((t, c), (t, a), (t, b), (c, c), (c, a), (t, t))
    for slot, (left, right) in enumerate(pairs):
        put_block(core, keep, send, slot, three(left, right, dot_nt))


def far_blocks(place, trial, large, small, after, before, keep, send):
    core, x = place[1], place[3]
    quarter = trial.shape[1] // NX

    def pair(ref, first):
        parts = [split(ref[:, quarter_at(x + first + k, quarter)]) for k in range(2)]
        return tuple(jnp.concatenate([parts[0][k], parts[1][k]], axis=1) for k in range(2))

    def products(me):
        big, little = split(large[...]), split(small[...])
        big_first = tuple(part[:, : 2 * quarter] for part in big)
        big_second = tuple(part[:, quarter:] for part in big)
        if me == 0:
            ta, tb, ta_cross, tb_cross, cross = little, big_second, little, big_first, 1
        else:
            ta, tb, ta_cross, tb_cross, cross = big_first, little, big_second, little, 2
        ca, cb = pair(after, cross), pair(before, cross)
        pairs = (
            (tb_cross, ca),
            (ta_cross, cb),
            (cb, ca),
            (tb_cross, ta_cross),
            (pair(trial, 1), ta),
            (pair(trial, 2), tb),
        )
        for slot, (left, right) in enumerate(pairs):
            put_block(core, keep, send, slot, three(left, right, dot_nt))

    for me in range(NC):
        pl.when(core == me)(functools.partial(products, me))


VMEM = pl.BlockSpec(memory_space=pltpu.VMEM)
SMEM = pl.BlockSpec(memory_space=pltpu.SMEM)


def tile_kernel(body, place, operands, block, flops):
    tiles = jax.ShapeDtypeStruct((NY, NZ, SLOTS, 8, 128), F32)
    return pl.pallas_call(
        body,
        out_shape=(tiles, tiles),
        in_specs=[SMEM] + [VMEM] * len(operands),
        out_specs=(VMEM, VMEM),
        compiler_params=pltpu.CompilerParams(vmem_limit_bytes=32 * 1024 * 1024),
        cost_estimate=pl.CostEstimate(
            flops=flops, bytes_accessed=6 * 1024 * 1024, transcendentals=0
        ),
    )(place, *operands)


def gram(c_old, c_trial, place):
    block, slab = c_old.shape
    quarter = slab // NX
    after = from_offset(c_old, "x", NX, 1)
    before = from_offset(c_old, "x", NX, -1)
    large, small = pl.pallas_call(
        messages,
        out_shape=(
            jax.ShapeDtypeStruct((block, 3 * quarter), F32),
            jax.ShapeDtypeStruct((block, 2 * quarter), F32),
        ),
        in_specs=[SMEM, VMEM],
        out_specs=(VMEM, VMEM),
    )(place, c_trial)
    large = mirrored(large, -1)
    small = mirrored(small, 1)
    flops = 6 * 6 * block * block * slab
    near, send = tile_kernel(
        near_blocks, place, (c_trial, c_old, after, before), block, flops
    )
    near, send, large, small = lax.optimization_barrier((near, send, large, small))
    near = sum_over_y(near + other_core(send))
    far, send = tile_kernel(
        far_blocks, place, (c_trial, large, small, after, before), block, flops // 2
    )
    to_far, far = lax.optimization_barrier((c_old, far))
    far_old = from_offset(to_far, "x", NX, 2)
    far = sum_over_y(far + other_core(send))
    return [c_old, after, far_old, before], jnp.concatenate([near, far], axis=1)


def sum_over_y(tiles):
    y = lax.axis_index("y")
    total = lax.dynamic_index_in_dim(tiles, y, 0, keepdims=False)
    for offset in range(1, NY):
        part = lax.dynamic_index_in_dim(tiles, (y + offset) % NY, 0, keepdims=False)
        total = total + from_offset(part, "y", NY, -offset)
    return total


def sum_over_z(tiles):
    return jnp.sum(lax.all_to_all(tiles, "z", 0, 0), axis=0)


def gather_over_z(tile):
    return lax.all_to_all(jnp.broadcast_to(tile[None], (NZ,) + tile.shape), "z", 0, 0)


def gather_all(tile):
    mine = gather_over_z(tile)
    parts = [mine] + [along(mine, False, r) for r in range(1, NY)]
    pieces = ring_forward(jnp.stack(parts[:2]), jnp.stack(parts[2:]), True)
    return pieces, [other_core(part) for part in pieces]


def constrain(place, *refs, block):
    count = PIECES
    own, other = refs[:count], refs[count : 2 * count]
    olds = refs[2 * count : 2 * count + NX]
    trial, c_new, mult = refs[2 * count + NX : 2 * count + NX + 3]
    e, s, n, xh, xl, sh, sl, wh, wl, q = refs[2 * count + NX + 3 :]
    total = NX * block
    y, core = place[0], place[1]
    lanes = 128
    wide = block // lanes
    core_rows = block // NC
    y_rows = core_rows // NY

    def put(value, which, shift, turn, z):
        group = lax.rem(y + turn, NY)
        inside = which * core_rows + group * y_rows + z // wide * 8
        r, after, before = shift, (shift + 1) % NX, (shift - 1) % NX
        targets = (
            (e, r, r),
            (e, r, after),
            (e, r, before),
            (s, r, r),
            (s, r, after),
            (n, r, r),
            (e, before, after),
            (s, after, r),
            (s, before, after),
            (n, before, after),
            (n, r, after),
            (n, r, before),
        )
        for k, (ref, row, col) in enumerate(targets):
            column = col * block + z % wide * lanes
            row = pl.multiple_of(row * block + inside, 8)
            ref[pl.ds(row, 8), column : column + lanes] = value[k]

    def assemble(me):
        for which, parts in enumerate((own, other) if me == 0 else (other, own)):
            for shift in range(NX):
                for turn in range(NY):
                    offset, at = (shift, turn) if which == 0 else (turn, shift)
                    for z in range(NZ):
                        value = parts[2 * offset + at // 2][at % 2, z]
                        put(value, which, shift, turn, z)

    for me in range(NC):
        pl.when(core == me)(functools.partial(assemble, me))

    def eye():
        rows = lax.broadcasted_iota(jnp.int32, (block, block), 0)
        cols = lax.broadcasted_iota(jnp.int32, (block, block), 1)
        return (rows == cols).astype(F32)

    def span(i):
        return slice(i * block, (i + 1) * block)

    def put_split(high_ref, low_ref, i, j, value):
        high, low = split(value)
        high_ref[span(i), span(j)], low_ref[span(i), span(j)] = high, low

    for i in range(NX):
        e[span(i), span(i)] = e[span(i), span(i)] - eye()
        far, spare = span((i + 2) % NX), span((i - 1) % NX)
        e[span(i), far] = e[span(i), far] + s[span(i), spare]
        start = eye() - n[span(i), span(i)]
        n[span(i), span(i)] = start
        put_split(xh, xl, i, i, 0.5 * start)
        put_split(sh, sl, i, i, s[span(i), span(i)])
        k = (i + 1) % NX
        put_split(sh, sl, i, k, s[span(i), span(k)])
        put_split(sh, sl, k, i, s[span(i), span(k)].T)
        for j in range(i):
            start = -(n[span(i), span(j)] + n[span(j), span(i)].T)
            n[span(i), span(j)] = start
            put_split(xh, xl, i, j, 0.5 * start)
            start = start.T
            n[span(j), span(i)] = start
            put_split(xh, xl, j, i, 0.5 * start)
            if i - j == 2:
                value = s[span(i), span(j)] + s[span(j), span(i)].T
                put_split(sh, sl, i, j, value)
                put_split(sh, sl, j, i, value.T)

    def columns(i):
        return pl.ds(pl.multiple_of(i * block, block), block)

    for sweep in range(ITERS - 2):

        def inner(i, carry):
            cols = columns(i)
            value = three((xh[...], xl[...]), (sh[:, cols], sl[:, cols]))
            high, low = split(-e[:, cols] - 0.5 * value)
            wh[:, cols], wl[:, cols] = high, low
            return carry

        lax.fori_loop(0, NX, inner, 0)

        def outer(i, carry):
            cols = columns(i)
            q[:total, cols] = three((wh[...], wl[...]), (xh[:, cols], xl[:, cols]))
            return carry

        lax.fori_loop(0, NX, outer, 0)
        for i in range(NX):
            for j in range(i + 1):
                value = 0.5 * (n[span(i), span(j)] + (q[span(i), span(j)] + q[span(j), span(i)].T))
                high, low = split(value)
                xh[span(i), span(j)], xl[span(i), span(j)] = high, low
                if i != j:
                    high, low = split(value.T)
                    xh[span(j), span(i)], xl[span(j), span(i)] = high, low

    row = (xh[:block], xl[:block])
    for j in range(NX):
        value = three(row, (sh[:, span(j)], sl[:, span(j)]))
        high, low = split(-e[:block, span(j)] - value)
        wh[:block, span(j)], wl[:block, span(j)] = high, low
    weight = (wh[:block], wl[:block])
    for j in range(NX):
        value = three(weight, (xh[:, span(j)], xl[:, span(j)]))
        value = value - three(row, split(e[span(j)]), dot_nt)
        q[:block, span(j)] = 0.5 * (n[:block, span(j)] + value)
    for j in range(NX):
        high, low = split(q[:block, span(j)])
        wh[:block, span(j)], wl[:block, span(j)] = high, low
        q[pl.ds(block + j * block, block), :block] = q[:block, span(j)].T
    begin = place[2]
    mult[...] = q[pl.ds(pl.multiple_of(block + begin, 16), mult.shape[0]), :block]
    value = trial[...]
    for j in range(NX):
        value = value + three((wh[:block, span(j)], wl[:block, span(j)]), split(olds[j][...]))
    c_new[...] = value


def local(c_old, c_trial):
    block, slab = c_old.shape
    total = block * NX
    x, y, z, core = (lax.axis_index(name) for name in ("x", "y", "z", "core"))
    grid_place = (z * NY + y) * NC + core
    tile_rows = total // (NZ * NY * NC)
    begin = (grid_place * tile_rows - x * block) % total
    place = jnp.stack([y, core, begin, x]).astype(jnp.int32)
    old_parts, tiles = gram(c_old, c_trial, place)
    tile = sum_over_z(tiles) * (1.0 / (slab * NC * NY * NZ))
    tile, old_parts[2] = lax.optimization_barrier((tile, old_parts[2]))
    own, other = gather_all(tile)
    wide = pltpu.VMEM((total, total), F32)
    thin = pltpu.VMEM((total, total), BF16)
    count = 2 * PIECES + NX + 1
    return pl.pallas_call(
        functools.partial(constrain, block=block),
        out_shape=(
            jax.ShapeDtypeStruct((block, slab), F32),
            jax.ShapeDtypeStruct((tile_rows, block), F32),
        ),
        in_specs=[SMEM] + [VMEM] * count,
        out_specs=(VMEM, VMEM),
        scratch_shapes=[wide] * 3 + [thin] * 6 + [pltpu.VMEM((total + block, total), F32)],
        compiler_params=pltpu.CompilerParams(vmem_limit_bytes=VMEM_BYTES),
        cost_estimate=pl.CostEstimate(
            flops=40 * total**3, bytes_accessed=24 * 1024 * 1024, transcendentals=0
        ),
    )(place, *own, *other, *old_parts, c_trial)


def solution(mesh):
    fine = Mesh(mesh.devices.reshape(NZ, NY, NC, NX), ("z", "y", "core", "x"))
    grid = ("z", "y", "core")
    return jax.shard_map(
        local,
        mesh=fine,
        in_specs=(P("x", grid), P("x", grid)),
        out_specs=(P("x", grid), P(grid, "x")),
        check_vma=False,
    )
```

```python
import functools

import jax
import jax.numpy as jnp
from jax import lax
from jax.experimental import pallas as pl
from jax.experimental.pallas import tpu as pltpu
from jax.sharding import Mesh, PartitionSpec as P

ITERS = 4
NX, NY, NZ, NC = 4, 4, 8, 2
BF16, F32 = jnp.bfloat16, jnp.float32
PIECES = 8
SLOTS = 6
VMEM_BYTES = 43 * 1024 * 1024


def from_offset(value, axis, size, offset):
    return lax.ppermute(value, axis, [((i + offset) % size, i) for i in range(size)])


MESH_AXES = ("z", "y", "core", "x")


def along(value, turned, offset):
    def source_of(z, y, core, x):
        if (core == 0) != turned:
            return z, (y + offset) % NY, core, x
        return z, y, core, (x + offset) % NX

    return from_source(value, source_of)


def mirrored(value, offset):
    def source_of(z, y, core, x):
        return z, y, core, (x + (offset if core == 0 else -offset)) % NX

    return from_source(value, source_of)


def from_source(value, source_of):
    pairs = []
    for z in range(NZ):
        for y in range(NY):
            for core in range(NC):
                for x in range(NX):
                    source = source_of(z, y, core, x)
                    places = (source, (z, y, core, x))
                    flat = [((a * NY + b) * NC + c) * NX + d for a, b, c, d in places]
                    pairs.append(tuple(flat))
    return lax.ppermute(value, MESH_AXES, pairs)


def ring_forward(top, low, turned):
    after_top = along(top, turned, 1)
    before_low = along(low, turned, -1)
    after_low = along(low, turned, 1)
    before_top = along(top, turned, -1)
    far_top = along(after_top, turned, 1)
    far_low = along(before_low, turned, -1)
    return [top, low, after_top, after_low, far_top, far_low, before_top, before_low]


def other_core(value):
    return from_offset(value, "core", NC, 1)


def split(value):
    high = value.astype(BF16)
    return high, (value - high.astype(F32)).astype(BF16)


def dot(left, right):
    return jnp.dot(left, right, preferred_element_type=F32)


def dot_nt(left, right):
    return lax.dot_general(left, right, (((1,), (1,)), ((), ())), preferred_element_type=F32)


def three(left, right, form=dot):
    return form(left[0], right[0]) + (form(left[0], right[1]) + form(left[1], right[0]))


def messages(place, trial, large, small):
    core, x = place[1], place[3]
    quarter = trial.shape[1] // NX
    first = x + 2 - 2 * core
    second = x + 3 * core
    for ref, begin, count in ((large, first, 3), (small, second, 2)):
        for k in range(count):
            ref[:, k * quarter : (k + 1) * quarter] = trial[:, quarter_at(begin + k, quarter)]


def quarter_at(index, quarter):
    return pl.ds(pl.multiple_of(lax.rem(index, NX) * quarter, quarter), quarter)


def put_block(core, keep, send, slot, value):
    half = value.shape[0] // NC
    first = core == 0
    kept = jnp.where(first, value[:half], value[half:])
    sent = jnp.where(first, value[half:], value[:half])
    wide = value.shape[1] // 128
    deep = NZ // wide
    for y in range(NY):
        for z in range(NZ):
            rows = slice((y * deep + z // wide) * 8, (y * deep + z // wide) * 8 + 8)
            cols = slice(z % wide * 128, z % wide * 128 + 128)
            keep[y, z, slot] = kept[rows, cols]
            send[y, z, slot] = sent[rows, cols]


def near_blocks(place, trial, old, after, before, keep, send):
    core = place[1]
    t, c, a, b = (split(ref[...]) for ref in (trial, old, after, before))
    pairs = ((t, c), (t, a), (t, b), (c, c), (c, a), (t, t))
    for slot, (left, right) in enumerate(pairs):
        put_block(core, keep, send, slot, three(left, right, dot_nt))


def far_blocks(place, trial, large, small, after, before, keep, send):
    core, x = place[1], place[3]
    quarter = trial.shape[1] // NX

    def pair(ref, first):
        parts = [split(ref[:, quarter_at(x + first + k, quarter)]) for k in range(2)]
        return tuple(jnp.concatenate([parts[0][k], parts[1][k]], axis=1) for k in range(2))

    def products(me):
        big, little = split(large[...]), split(small[...])
        big_first = tuple(part[:, : 2 * quarter] for part in big)
        big_second = tuple(part[:, quarter:] for part in big)
        if me == 0:
            ta, tb, ta_cross, tb_cross, cross = little, big_second, little, big_first, 1
        else:
            ta, tb, ta_cross, tb_cross, cross = big_first, little, big_second, little, 2
        ca, cb = pair(after, cross), pair(before, cross)
        pairs = (
            (tb_cross, ca),
            (ta_cross, cb),
            (cb, ca),
            (tb_cross, ta_cross),
            (pair(trial, 1), ta),
            (pair(trial, 2), tb),
        )
        for slot, (left, right) in enumerate(pairs):
            put_block(core, keep, send, slot, three(left, right, dot_nt))

    for me in range(NC):
        pl.when(core == me)(functools.partial(products, me))


VMEM = pl.BlockSpec(memory_space=pltpu.VMEM)
SMEM = pl.BlockSpec(memory_space=pltpu.SMEM)


def tile_kernel(body, place, operands, block, flops):
    tiles = jax.ShapeDtypeStruct((NY, NZ, SLOTS, 8, 128), F32)
    return pl.pallas_call(
        body,
        out_shape=(tiles, tiles),
        in_specs=[SMEM] + [VMEM] * len(operands),
        out_specs=(VMEM, VMEM),
        compiler_params=pltpu.CompilerParams(vmem_limit_bytes=32 * 1024 * 1024),
        cost_estimate=pl.CostEstimate(
            flops=flops, bytes_accessed=6 * 1024 * 1024, transcendentals=0
        ),
    )(place, *operands)


def gram(c_old, c_trial, place):
    block, slab = c_old.shape
    quarter = slab // NX
    after = from_offset(c_old, "x", NX, 1)
    before = from_offset(c_old, "x", NX, -1)
    large, small = pl.pallas_call(
        messages,
        out_shape=(
            jax.ShapeDtypeStruct((block, 3 * quarter), F32),
            jax.ShapeDtypeStruct((block, 2 * quarter), F32),
        ),
        in_specs=[SMEM, VMEM],
        out_specs=(VMEM, VMEM),
    )(place, c_trial)
    large = mirrored(large, -1)
    small = mirrored(small, 1)
    flops = 6 * 6 * block * block * slab
    near, send = tile_kernel(
        near_blocks, place, (c_trial, c_old, after, before), block, flops
    )
    near, send, large, small = lax.optimization_barrier((near, send, large, small))
    near = sum_over_y(near + other_core(send))
    far, send = tile_kernel(
        far_blocks, place, (c_trial, large, small, after, before), block, flops // 2
    )
    to_far, far = lax.optimization_barrier((c_old, far))
    far_old = from_offset(to_far, "x", NX, 2)
    far = sum_over_y(far + other_core(send))
    return [c_old, after, far_old, before], jnp.concatenate([near, far], axis=1)


def sum_over_y(tiles):
    y = lax.axis_index("y")
    total = lax.dynamic_index_in_dim(tiles, y, 0, keepdims=False)
    for offset in range(1, NY):
        part = lax.dynamic_index_in_dim(tiles, (y + offset) % NY, 0, keepdims=False)
        total = total + from_offset(part, "y", NY, -offset)
    return total


def sum_over_z(tiles):
    return jnp.sum(lax.all_to_all(tiles, "z", 0, 0), axis=0)


def gather_over_z(tile):
    return lax.all_to_all(jnp.broadcast_to(tile[None], (NZ,) + tile.shape), "z", 0, 0)


def gather_all(tile):
    mine = gather_over_z(tile)
    parts = [mine] + [along(mine, False, r) for r in range(1, NY)]
    pieces = ring_forward(jnp.stack(parts[:2]), jnp.stack(parts[2:]), True)
    top, low, after_top, after_low, far_top, far_low, before_top, before_low = pieces
    top, low, after_top, before_low = lax.optimization_barrier((top, low, after_top, before_low))
    after_top, before_low, after_low, before_top = lax.optimization_barrier(
        (after_top, before_low, after_low, before_top)
    )
    swapped = (top, low, after_top, after_low, far_top, far_low, before_top, before_low)
    return pieces, [other_core(part) for part in swapped]


def constrain(place, *refs, block):
    count = PIECES
    own, other = refs[:count], refs[count : 2 * count]
    olds = refs[2 * count : 2 * count + NX]
    trial, c_new, mult = refs[2 * count + NX : 2 * count + NX + 3]
    e, s, n, xh, xl, sh, sl, wh, wl, q = refs[2 * count + NX + 3 :]
    total = NX * block
    y, core = place[0], place[1]
    lanes = 128
    wide = block // lanes
    core_rows = block // NC
    y_rows = core_rows // NY

    def put(value, which, shift, turn, z):
        group = lax.rem(y + turn, NY)
        inside = which * core_rows + group * y_rows + z // wide * 8
        r, after, before = shift, (shift + 1) % NX, (shift - 1) % NX
        targets = (
            (e, r, r),
            (e, r, after),
            (e, r, before),
            (s, r, r),
            (s, r, after),
            (n, r, r),
            (e, before, after),
            (s, after, r),
            (s, before, after),
            (n, before, after),
            (n, r, after),
            (n, r, before),
        )
        for k, (ref, row, col) in enumerate(targets):
            column = col * block + z % wide * lanes
            row = pl.multiple_of(row * block + inside, 8)
            ref[pl.ds(row, 8), column : column + lanes] = value[k]

    def assemble(me):
        for which, parts in enumerate((own, other) if me == 0 else (other, own)):
            for shift in range(NX):
                for turn in range(NY):
                    offset, at = (shift, turn) if which == 0 else (turn, shift)
                    for z in range(NZ):
                        value = parts[2 * offset + at // 2][at % 2, z]
                        put(value, which, shift, turn, z)

    for me in range(NC):
        pl.when(core == me)(functools.partial(assemble, me))

    def eye():
        rows = lax.broadcasted_iota(jnp.int32, (block, block), 0)
        cols = lax.broadcasted_iota(jnp.int32, (block, block), 1)
        return (rows == cols).astype(F32)

    def span(i):
        return slice(i * block, (i + 1) * block)

    def put_split(high_ref, low_ref, i, j, value):
        high, low = split(value)
        high_ref[span(i), span(j)], low_ref[span(i), span(j)] = high, low

    for i in range(NX):
        e[span(i), span(i)] = e[span(i), span(i)] - eye()
        far, spare = span((i + 2) % NX), span((i - 1) % NX)
        e[span(i), far] = e[span(i), far] + s[span(i), spare]
        start = eye() - n[span(i), span(i)]
        n[span(i), span(i)] = start
        put_split(xh, xl, i, i, 0.5 * start)
        put_split(sh, sl, i, i, s[span(i), span(i)])
        k = (i + 1) % NX
        put_split(sh, sl, i, k, s[span(i), span(k)])
        put_split(sh, sl, k, i, s[span(i), span(k)].T)
        for j in range(i):
            start = -(n[span(i), span(j)] + n[span(j), span(i)].T)
            n[span(i), span(j)] = start
            put_split(xh, xl, i, j, 0.5 * start)
            start = start.T
            n[span(j), span(i)] = start
            put_split(xh, xl, j, i, 0.5 * start)
            if i - j == 2:
                value = s[span(i), span(j)] + s[span(j), span(i)].T
                put_split(sh, sl, i, j, value)
                put_split(sh, sl, j, i, value.T)

    def columns(i):
        return pl.ds(pl.multiple_of(i * block, block), block)

    for sweep in range(ITERS - 2):

        def inner(i, carry):
            cols = columns(i)
            value = three((xh[...], xl[...]), (sh[:, cols], sl[:, cols]))
            high, low = split(-e[:, cols] - 0.5 * value)
            wh[:, cols], wl[:, cols] = high, low
            return carry

        lax.fori_loop(0, NX, inner, 0, unroll=True)

        def outer(i, carry):
            cols = columns(i)
            q[:total, cols] = three((wh[...], wl[...]), (xh[:, cols], xl[:, cols]))
            return carry

        lax.fori_loop(0, NX, outer, 0, unroll=True)
        for i in range(NX):
            for j in range(i + 1):
                value = 0.5 * (n[span(i), span(j)] + (q[span(i), span(j)] + q[span(j), span(i)].T))
                high, low = split(value)
                xh[span(i), span(j)], xl[span(i), span(j)] = high, low
                if i != j:
                    high, low = split(value.T)
                    xh[span(j), span(i)], xl[span(j), span(i)] = high, low

    row = (xh[:block], xl[:block])
    for j in range(NX):
        value = three(row, (sh[:, span(j)], sl[:, span(j)]))
        high, low = split(-e[:block, span(j)] - value)
        wh[:block, span(j)], wl[:block, span(j)] = high, low
    weight = (wh[:block], wl[:block])
    for j in range(NX):
        value = three(weight, (xh[:, span(j)], xl[:, span(j)]))
        value = value - three(row, split(e[span(j)]), dot_nt)
        q[:block, span(j)] = 0.5 * (n[:block, span(j)] + value)
    for j in range(NX):
        high, low = split(q[:block, span(j)])
        wh[:block, span(j)], wl[:block, span(j)] = high, low
        q[pl.ds(block + j * block, block), :block] = q[:block, span(j)].T
    begin = place[2]
    mult[...] = q[pl.ds(pl.multiple_of(block + begin, 16), mult.shape[0]), :block]
    value = trial[...]
    for j in range(NX):
        value = value + three((wh[:block, span(j)], wl[:block, span(j)]), split(olds[j][...]))
    c_new[...] = value


def local(c_old, c_trial):
    block, slab = c_old.shape
    total = block * NX
    x, y, z, core = (lax.axis_index(name) for name in ("x", "y", "z", "core"))
    grid_place = (z * NY + y) * NC + core
    tile_rows = total // (NZ * NY * NC)
    begin = (grid_place * tile_rows - x * block) % total
    place = jnp.stack([y, core, begin, x]).astype(jnp.int32)
    old_parts, tiles = gram(c_old, c_trial, place)
    tile = sum_over_z(tiles) * (1.0 / (slab * NC * NY * NZ))
    tile, old_parts[2] = lax.optimization_barrier((tile, old_parts[2]))
    own, other = gather_all(tile)
    wide = pltpu.VMEM((total, total), F32)
    thin = pltpu.VMEM((total, total), BF16)
    count = 2 * PIECES + NX + 1
    return pl.pallas_call(
        functools.partial(constrain, block=block),
        out_shape=(
            jax.ShapeDtypeStruct((block, slab), F32),
            jax.ShapeDtypeStruct((tile_rows, block), F32),
        ),
        in_specs=[SMEM] + [VMEM] * count,
        out_specs=(VMEM, VMEM),
        scratch_shapes=[wide] * 3 + [thin] * 6 + [pltpu.VMEM((total + block, total), F32)],
        compiler_params=pltpu.CompilerParams(vmem_limit_bytes=VMEM_BYTES),
        cost_estimate=pl.CostEstimate(
            flops=40 * total**3, bytes_accessed=24 * 1024 * 1024, transcendentals=0
        ),
    )(place, *own, *other, *old_parts, c_trial)


def solution(mesh):
    fine = Mesh(mesh.devices.reshape(NZ, NY, NC, NX), ("z", "y", "core", "x"))
    grid = ("z", "y", "core")
    return jax.shard_map(
        local,
        mesh=fine,
        in_specs=(P("x", grid), P("x", grid)),
        out_specs=(P("x", grid), P(grid, "x")),
        check_vma=False,
    )
```

```python
import functools

import jax
import jax.numpy as jnp
from jax import lax
from jax.experimental import pallas as pl
from jax.experimental.pallas import tpu as pltpu
from jax.sharding import Mesh, PartitionSpec as P

ITERS = 4
NX, NY, NZ, NC = 4, 4, 8, 2
BF16, F32 = jnp.bfloat16, jnp.float32
PIECES = 8
SLOTS = 6
VMEM_BYTES = 43 * 1024 * 1024


def from_offset(value, axis, size, offset):
    return lax.ppermute(value, axis, [((i + offset) % size, i) for i in range(size)])


MESH_AXES = ("z", "y", "core", "x")


def along(value, turned, offset):
    def source_of(z, y, core, x):
        if (core == 0) != turned:
            return z, (y + offset) % NY, core, x
        return z, y, core, (x + offset) % NX

    return from_source(value, source_of)


def mirrored(value, offset):
    def source_of(z, y, core, x):
        return z, y, core, (x + (offset if core == 0 else -offset)) % NX

    return from_source(value, source_of)


def from_source(value, source_of):
    pairs = []
    for z in range(NZ):
        for y in range(NY):
            for core in range(NC):
                for x in range(NX):
                    source = source_of(z, y, core, x)
                    places = (source, (z, y, core, x))
                    flat = [((a * NY + b) * NC + c) * NX + d for a, b, c, d in places]
                    pairs.append(tuple(flat))
    return lax.ppermute(value, MESH_AXES, pairs)


def ring_forward(top, low, turned):
    after_top = along(top, turned, 1)
    before_low = along(low, turned, -1)
    after_low = along(low, turned, 1)
    before_top = along(top, turned, -1)
    far_top = along(after_top, turned, 1)
    far_low = along(before_low, turned, -1)
    return [top, low, after_top, after_low, far_top, far_low, before_top, before_low]


def other_core(value):
    return from_offset(value, "core", NC, 1)


def split(value):
    high = value.astype(BF16)
    return high, (value - high.astype(F32)).astype(BF16)


def dot(left, right):
    return jnp.dot(left, right, preferred_element_type=F32)


def dot_nt(left, right):
    return lax.dot_general(left, right, (((1,), (1,)), ((), ())), preferred_element_type=F32)


def three(left, right, form=dot):
    return form(left[0], right[0]) + (form(left[0], right[1]) + form(left[1], right[0]))


def messages(place, trial, large, small):
    core, x = place[1], place[3]
    quarter = trial.shape[1] // NX
    first = x + 2 - 2 * core
    second = x + 3 * core
    for ref, begin, count in ((large, first, 3), (small, second, 2)):
        for k in range(count):
            ref[:, k * quarter : (k + 1) * quarter] = trial[:, quarter_at(begin + k, quarter)]


def quarter_at(index, quarter):
    return pl.ds(pl.multiple_of(lax.rem(index, NX) * quarter, quarter), quarter)


def put_block(core, keep, send, slot, value):
    half = value.shape[0] // NC
    first = core == 0
    kept = jnp.where(first, value[:half], value[half:])
    sent = jnp.where(first, value[half:], value[:half])
    wide = value.shape[1] // 128
    deep = NZ // wide
    for y in range(NY):
        for z in range(NZ):
            rows = slice((y * deep + z // wide) * 8, (y * deep + z // wide) * 8 + 8)
            cols = slice(z % wide * 128, z % wide * 128 + 128)
            keep[y, z, slot] = kept[rows, cols]
            send[y, z, slot] = sent[rows, cols]


def near_blocks(place, trial, old, after, before, keep, send):
    core = place[1]
    t, c, a, b = (split(ref[...]) for ref in (trial, old, after, before))
    pairs = ((t, c), (t, a), (t, b), (c, c), (c, a), (t, t))
    for slot, (left, right) in enumerate(pairs):
        put_block(core, keep, send, slot, three(left, right, dot_nt))


def far_blocks(place, trial, large, small, after, before, keep, send):
    core, x = place[1], place[3]
    quarter = trial.shape[1] // NX

    def pair(ref, first):
        parts = [split(ref[:, quarter_at(x + first + k, quarter)]) for k in range(2)]
        return tuple(jnp.concatenate([parts[0][k], parts[1][k]], axis=1) for k in range(2))

    def products(me):
        big, little = split(large[...]), split(small[...])
        big_first = tuple(part[:, : 2 * quarter] for part in big)
        big_second = tuple(part[:, quarter:] for part in big)
        if me == 0:
            ta, tb, ta_cross, tb_cross, cross = little, big_second, little, big_first, 1
        else:
            ta, tb, ta_cross, tb_cross, cross = big_first, little, big_second, little, 2
        ca, cb = pair(after, cross), pair(before, cross)
        pairs = (
            (tb_cross, ca),
            (ta_cross, cb),
            (cb, ca),
            (tb_cross, ta_cross),
            (pair(trial, 1), ta),
            (pair(trial, 2), tb),
        )
        for slot, (left, right) in enumerate(pairs):
            put_block(core, keep, send, slot, three(left, right, dot_nt))

    for me in range(NC):
        pl.when(core == me)(functools.partial(products, me))


VMEM = pl.BlockSpec(memory_space=pltpu.VMEM)
SMEM = pl.BlockSpec(memory_space=pltpu.SMEM)


def tile_kernel(body, place, operands, block, flops):
    tiles = jax.ShapeDtypeStruct((NY, NZ, SLOTS, 8, 128), F32)
    return pl.pallas_call(
        body,
        out_shape=(tiles, tiles),
        in_specs=[SMEM] + [VMEM] * len(operands),
        out_specs=(VMEM, VMEM),
        compiler_params=pltpu.CompilerParams(vmem_limit_bytes=32 * 1024 * 1024),
        cost_estimate=pl.CostEstimate(
            flops=flops, bytes_accessed=6 * 1024 * 1024, transcendentals=0
        ),
    )(place, *operands)


def gram(c_old, c_trial, place):
    block, slab = c_old.shape
    quarter = slab // NX
    after = from_offset(c_old, "x", NX, 1)
    before = from_offset(c_old, "x", NX, -1)
    large, small = pl.pallas_call(
        messages,
        out_shape=(
            jax.ShapeDtypeStruct((block, 3 * quarter), F32),
            jax.ShapeDtypeStruct((block, 2 * quarter), F32),
        ),
        in_specs=[SMEM, VMEM],
        out_specs=(VMEM, VMEM),
    )(place, c_trial)
    large = mirrored(large, -1)
    small = mirrored(small, 1)
    flops = 6 * 6 * block * block * slab
    near, send = tile_kernel(
        near_blocks, place, (c_trial, c_old, after, before), block, flops
    )
    near, send, large, small = lax.optimization_barrier((near, send, large, small))
    near = sum_over_y(near + other_core(send))
    far, send = tile_kernel(
        far_blocks, place, (c_trial, large, small, after, before), block, flops // 2
    )
    to_far, far = lax.optimization_barrier((c_old, far))
    far_old = from_offset(to_far, "x", NX, 2)
    far = sum_over_y(far + other_core(send))
    return [c_old, after, far_old, before], jnp.concatenate([near, far], axis=1)


def sum_over_y(tiles):
    y = lax.axis_index("y")
    total = lax.dynamic_index_in_dim(tiles, y, 0, keepdims=False)
    for offset in range(1, NY):
        part = lax.dynamic_index_in_dim(tiles, (y + offset) % NY, 0, keepdims=False)
        total = total + from_offset(part, "y", NY, -offset)
    return total


def sum_over_z(tiles):
    return jnp.sum(lax.all_to_all(tiles, "z", 0, 0), axis=0)


def gather_over_z(tile):
    return lax.all_to_all(jnp.broadcast_to(tile[None], (NZ,) + tile.shape), "z", 0, 0)


def gather_all(tile):
    mine = gather_over_z(tile)
    parts = [mine] + [along(mine, False, r) for r in range(1, NY)]
    pieces = ring_forward(jnp.stack(parts[:2]), jnp.stack(parts[2:]), True)
    return pieces, [other_core(part) for part in pieces]


def constrain(place, *refs, block):
    count = PIECES
    own, other = refs[:count], refs[count : 2 * count]
    olds = refs[2 * count : 2 * count + NX]
    trial, c_new, mult = refs[2 * count + NX : 2 * count + NX + 3]
    e, s, n, xh, xl, sh, sl, wh, wl, q = refs[2 * count + NX + 3 :]
    total = NX * block
    y, core = place[0], place[1]
    lanes = 128
    wide = block // lanes
    core_rows = block // NC
    y_rows = core_rows // NY

    def put(value, which, shift, turn, z):
        group = lax.rem(y + turn, NY)
        inside = which * core_rows + group * y_rows + z // wide * 8
        r, after, before = shift, (shift + 1) % NX, (shift - 1) % NX
        targets = (
            (e, r, r),
            (e, r, after),
            (e, r, before),
            (s, r, r),
            (s, r, after),
            (n, r, r),
            (e, before, after),
            (s, after, r),
            (s, before, after),
            (n, before, after),
            (n, r, after),
            (n, r, before),
        )
        for k, (ref, row, col) in enumerate(targets):
            column = col * block + z % wide * lanes
            row = pl.multiple_of(row * block + inside, 8)
            ref[pl.ds(row, 8), column : column + lanes] = value[k]

    def assemble(me):
        for which, parts in enumerate((own, other) if me == 0 else (other, own)):
            for shift in range(NX):
                for turn in range(NY):
                    offset, at = (shift, turn) if which == 0 else (turn, shift)
                    for z in range(NZ):
                        value = parts[2 * offset + at // 2][at % 2, z]
                        put(value, which, shift, turn, z)

    for me in range(NC):
        pl.when(core == me)(functools.partial(assemble, me))

    def eye():
        rows = lax.broadcasted_iota(jnp.int32, (block, block), 0)
        cols = lax.broadcasted_iota(jnp.int32, (block, block), 1)
        return (rows == cols).astype(F32)

    def span(i):
        return slice(i * block, (i + 1) * block)

    def put_split(high_ref, low_ref, i, j, value):
        high, low = split(value)
        high_ref[span(i), span(j)], low_ref[span(i), span(j)] = high, low

    for i in range(NX):
        e[span(i), span(i)] = e[span(i), span(i)] - eye()
        far, spare = span((i + 2) % NX), span((i - 1) % NX)
        e[span(i), far] = e[span(i), far] + s[span(i), spare]
        start = eye() - n[span(i), span(i)]
        n[span(i), span(i)] = start
        put_split(xh, xl, i, i, 0.5 * start)
        put_split(sh, sl, i, i, s[span(i), span(i)])
        k = (i + 1) % NX
        put_split(sh, sl, i, k, s[span(i), span(k)])
        put_split(sh, sl, k, i, s[span(i), span(k)].T)
        for j in range(i):
            start = -(n[span(i), span(j)] + n[span(j), span(i)].T)
            n[span(i), span(j)] = start
            put_split(xh, xl, i, j, 0.5 * start)
            start = start.T
            n[span(j), span(i)] = start
            put_split(xh, xl, j, i, 0.5 * start)
            if i - j == 2:
                value = s[span(i), span(j)] + s[span(j), span(i)].T
                put_split(sh, sl, i, j, value)
                put_split(sh, sl, j, i, value.T)

    def columns(i):
        return pl.ds(pl.multiple_of(i * block, block), block)

    for sweep in range(ITERS - 2):

        def inner(i, carry):
            cols = columns(i)
            value = three((xh[...], xl[...]), (sh[:, cols], sl[:, cols]))
            high, low = split(-e[:, cols] - 0.5 * value)
            wh[:, cols], wl[:, cols] = high, low
            return carry

        lax.fori_loop(0, NX, inner, 0, unroll=True)

        def outer(i, carry):
            cols = columns(i)
            q[:total, cols] = three((wh[...], wl[...]), (xh[:, cols], xl[:, cols]))
            return carry

        lax.fori_loop(0, NX, outer, 0, unroll=True)
        for i in range(NX):
            for j in range(i + 1):
                value = 0.5 * (n[span(i), span(j)] + (q[span(i), span(j)] + q[span(j), span(i)].T))
                high, low = split(value)
                xh[span(i), span(j)], xl[span(i), span(j)] = high, low
                if i != j:
                    high, low = split(value.T)
                    xh[span(j), span(i)], xl[span(j), span(i)] = high, low

    row = (xh[:block], xl[:block])
    for j in range(NX):
        value = three(row, (sh[:, span(j)], sl[:, span(j)]))
        high, low = split(-e[:block, span(j)] - value)
        wh[:block, span(j)], wl[:block, span(j)] = high, low
    weight = (wh[:block], wl[:block])
    for j in range(NX):
        value = three(weight, (xh[:, span(j)], xl[:, span(j)]))
        value = value - three(row, split(e[span(j)]), dot_nt)
        q[:block, span(j)] = 0.5 * (n[:block, span(j)] + value)
    for j in range(NX):
        high, low = split(q[:block, span(j)])
        wh[:block, span(j)], wl[:block, span(j)] = high, low
        q[pl.ds(block + j * block, block), :block] = q[:block, span(j)].T
    begin = place[2]
    mult[...] = q[pl.ds(pl.multiple_of(block + begin, 16), mult.shape[0]), :block]
    value = trial[...]
    for j in range(NX):
        value = value + three((wh[:block, span(j)], wl[:block, span(j)]), split(olds[j][...]))
    c_new[...] = value


def local(c_old, c_trial):
    block, slab = c_old.shape
    total = block * NX
    x, y, z, core = (lax.axis_index(name) for name in ("x", "y", "z", "core"))
    grid_place = (z * NY + y) * NC + core
    tile_rows = total // (NZ * NY * NC)
    begin = (grid_place * tile_rows - x * block) % total
    place = jnp.stack([y, core, begin, x]).astype(jnp.int32)
    old_parts, tiles = gram(c_old, c_trial, place)
    tile = sum_over_z(tiles) * (1.0 / (slab * NC * NY * NZ))
    tile, old_parts[2] = lax.optimization_barrier((tile, old_parts[2]))
    own, other = gather_all(tile)
    wide = pltpu.VMEM((total, total), F32)
    thin = pltpu.VMEM((total, total), BF16)
    count = 2 * PIECES + NX + 1
    return pl.pallas_call(
        functools.partial(constrain, block=block),
        out_shape=(
            jax.ShapeDtypeStruct((block, slab), F32),
            jax.ShapeDtypeStruct((tile_rows, block), F32),
        ),
        in_specs=[SMEM] + [VMEM] * count,
        out_specs=(VMEM, VMEM),
        scratch_shapes=[wide] * 3 + [thin] * 6 + [pltpu.VMEM((total + block, total), F32)],
        compiler_params=pltpu.CompilerParams(vmem_limit_bytes=VMEM_BYTES),
        cost_estimate=pl.CostEstimate(
            flops=40 * total**3, bytes_accessed=24 * 1024 * 1024, transcendentals=0
        ),
    )(place, *own, *other, *old_parts, c_trial)


def solution(mesh):
    fine = Mesh(mesh.devices.reshape(NZ, NY, NC, NX), ("z", "y", "core", "x"))
    grid = ("z", "y", "core")
    return jax.shard_map(
        local,
        mesh=fine,
        in_specs=(P("x", grid), P("x", grid)),
        out_specs=(P("x", grid), P(grid, "x")),
        check_vma=False,
    )
```
